256 devices in a mesh: dp: 32 (over z, y), group: 8 (over x, core).
Axes of the slice: x: 4, y: 4, z: 8, core: 2. Of those that a mesh axis runs over, the one named last changes fastest.
Arguments:
- embeddings: bfloat16 [262144, 768], P(('dp', 'group')), may hold values from -6 to 6
- coarse_label: int32 [262144], P(('dp', 'group')), may hold values from 0 to 8191, as said below
- fine_label: int32 [262144], P(('dp', 'group')), may hold values from 0 to 63
- slot_table: int32 [8192], replicated, may hold values from 0 to 8191, as said below
- coarse_means: bfloat16 [8192, 768], P(('dp', 'group')), may hold values from -3 to 3
- fine_means: bfloat16 [8192, 49152], P('dp', 'group'), may hold values from -3 to 3
Outputs:
- coarse_update: bfloat16 [8192, 768], P(('dp', 'group'))
- fine_update: bfloat16 [8192, 49152], P('dp', 'group')
- nearest_cost: float32 [262144], P(('dp', 'group'))
The draws below stay inside these ranges and needn't reach their ends.
Inputs may be any that keep to these rules, and one draw needn't show every extreme that they name: `coarse_label`: through slot_table, at most 128 of the 1024 rows of one device have clusters whose slots lie on one index of dp (slot s on index s // 256); in every draw one index of dp receives exactly 128 rows from every device. `slot_table`: A permutation: each slot holds exactly one cluster.
All inputs are finite; a program needn't handle non-finite values.
Results may differ from the reference program's by a relative error of at most 0.001.
Values may be sent and summed in bfloat16 or wider, within the bound.
A program may use at most 128 MiB of HBM per device.

```python
import math
import jax
import jax.numpy as jnp
from jax import lax

D = 768
SUB = 64
CL_DEV = 256
R_DEV = 1024
K1 = 8192
ROWS = 262144
CAP = 128


def routing_tables(key):
    base_key = jax.random.fold_in(key, 7177)
    perm_key, busy_key, owner_key, within_key = jax.random.split(base_key, 4)
    slot_of = jax.random.permutation(perm_key, K1).astype(jnp.int32)
    cluster_at = jnp.zeros((K1,), jnp.int32).at[slot_of].set(jnp.arange(K1, dtype=jnp.int32))
    owner_total = K1 // CL_DEV
    busiest = jax.random.randint(busy_key, (), 0, owner_total).astype(jnp.int32)
    remaining = R_DEV - CAP
    block_total = ROWS // R_DEV

    def one_block(block_key):
        first_key, second_key = jax.random.split(block_key)
        positions = jax.random.permutation(first_key, 2 * remaining)[:remaining].astype(jnp.int32)
        others = positions % (owner_total - 1)
        others = others + (others >= busiest).astype(jnp.int32)
        owners = jnp.concatenate([jnp.full((CAP,), busiest, jnp.int32), others])
        return jax.random.permutation(second_key, owners)
    owners = jax.vmap(one_block)(jax.random.split(owner_key, block_total)).reshape(ROWS)
    within = jax.random.randint(within_key, (ROWS,), 0, CL_DEV).astype(jnp.int32)
    slot_index = owners * CL_DEV + within
    return (slot_of, cluster_at[slot_index], slot_index)


def center_table(key):
    center_key = jax.random.fold_in(key, 9151)
    return 0.5 * jnp.clip(jax.random.normal(center_key, (K1, D), jnp.float32), -6.0, 6.0)


def nearby_slots(key):
    slot_of, labels, slot_index = routing_tables(key)
    mix_key = jax.random.fold_in(key, 3307)
    stray_key, other_key = jax.random.split(mix_key)
    stray = jax.random.randint(stray_key, (ROWS,), 0, 3) == 0
    other = jax.random.randint(other_key, (ROWS,), 0, K1).astype(jnp.int32)
    return jnp.where(stray, other, slot_index).astype(jnp.int32)


def draw_coarse_label(key, part):
    slot_of, labels, slot_index = routing_tables(key)
    return labels.astype(jnp.int32)


def draw_slot_table(key, part):
    slot_of, labels, slot_index = routing_tables(key)
    return slot_of.astype(jnp.int32)


def draw_coarse_means(key, part):
    return center_table(key).astype(jnp.bfloat16)


def draw_embeddings(key, part):
    centers = center_table(key)
    near = nearby_slots(key)
    noise_key = jax.random.fold_in(key, 5581)
    noise = 0.8 * jax.random.normal(noise_key, (ROWS, D), jnp.float32)
    rows = jnp.take(centers, near, axis=0) + noise
    return jnp.clip(rows, -6.0, 6.0).astype(jnp.bfloat16)


def place_ends(entries, rng, low, top_value):
    dims = entries.shape
    place = [jax.random.randint(jax.random.fold_in(rng, axis), (), 0, dims[axis]) for axis in range(len(dims))]
    entries = entries.at[tuple(place)].set(low)
    longest = dims.index(max(dims))
    place[longest] = (place[longest] + 1) % dims[longest]
    return entries.at[tuple(place)].set(top_value)


def block_scale(own_key, dims, cuts, least, largest):
    loudness, own = 1.0, jax.random.fold_in(own_key, 6)
    for dim, blocks in cuts:
        heights = jnp.exp(jax.random.uniform(jax.random.fold_in(own, dim), (blocks,), jnp.float32, least / len(cuts), largest / len(cuts)))
        loudness = loudness * jnp.repeat(heights, dims[dim] // blocks).reshape([-1 if axis == dim else 1 for axis in range(len(dims))])
    return loudness


def normal_values(key, shape, spread, most, cuts=(), kind=jnp.bfloat16):
    array = spread * jax.random.normal(key, shape, jnp.float32)
    if cuts:
        array = array * block_scale(key, shape, cuts, -0.22, 0.18)
    return jnp.clip(array, -most, most).astype(kind)


def setup_inputs(seed: int = 0) -> dict:
    key_of = jax.random.split(jax.random.key(seed), 7)
    embeddings = draw_embeddings(jax.random.fold_in(key_of[6], 71), 0)
    coarse_label = draw_coarse_label(jax.random.fold_in(key_of[6], 71), 0)
    fine_label = place_ends(jax.random.randint(key_of[2], (ROWS,), 0, SUB), jax.random.fold_in(key_of[2], 1), 0, SUB - 1).astype(jnp.int32)
    slot_table = draw_slot_table(jax.random.fold_in(key_of[6], 71), 0)
    coarse_means = draw_coarse_means(jax.random.fold_in(key_of[6], 71), 0)
    fine_means = normal_values(key_of[5], (K1, D * SUB), 0.5, 3.0, ((0, 32), (1, 8)))
    return dict(embeddings=embeddings, coarse_label=coarse_label, fine_label=fine_label, slot_table=slot_table, coarse_means=coarse_means, fine_means=fine_means)


def block_costs(block_rows, coarse_means):
    square_norms = jnp.sum(jnp.square(coarse_means.astype(jnp.float32)), axis=1)
    products = lax.dot_general(block_rows, coarse_means, (((1,), (1,)), ((), ())), preferred_element_type=jnp.float32)
    lowest = jnp.min(square_norms[None, :] - 2.0 * products, axis=1)
    own_norms = jnp.sum(jnp.square(block_rows.astype(jnp.float32)), axis=1)
    return (own_norms + lowest) / D


def reference(embeddings, coarse_label, fine_label, slot_table, coarse_means, fine_means):
    slot_index = jnp.take(slot_table, coarse_label).astype(jnp.int32)
    values = embeddings.astype(jnp.float32)
    ones_column = jnp.ones((ROWS,), jnp.float32)
    coarse_sum = jax.ops.segment_sum(values, slot_index, num_segments=K1)
    coarse_count = jax.ops.segment_sum(ones_column, slot_index, num_segments=K1)
    coarse_update = ((coarse_sum + coarse_means.astype(jnp.float32)) / (coarse_count[:, None] + 1.0)).astype(jnp.bfloat16)
    cell_index = (slot_index * SUB + fine_label).astype(jnp.int32)
    span = CL_DEV * SUB
    owner_count = K1 // CL_DEV

    def owner_block(inputs):
        owner_number, old_block = inputs
        shifted = cell_index - owner_number * span
        inside = (shifted >= 0) & (shifted < span)
        segment_index = jnp.where(inside, shifted, span).astype(jnp.int32)
        fine_sum = jax.ops.segment_sum(values, segment_index, num_segments=span + 1)[:span]
        fine_count = jax.ops.segment_sum(ones_column, segment_index, num_segments=span + 1)[:span]
        old_values = jnp.transpose(old_block.reshape(CL_DEV, D, SUB), (0, 2, 1)).reshape(span, D).astype(jnp.float32)
        fresh = ((fine_sum + old_values) / (fine_count[:, None] + 1.0)).astype(jnp.bfloat16)
        return jnp.transpose(fresh.reshape(CL_DEV, SUB, D), (0, 2, 1)).reshape(CL_DEV, D * SUB)

    fine_update = lax.map(owner_block, (jnp.arange(owner_count, dtype=jnp.int32), fine_means.reshape(owner_count, CL_DEV, D * SUB)))
    fine_update = fine_update.reshape(K1, D * SUB)
    block_size = math.gcd(ROWS, 1024)
    nearest_cost = lax.map(lambda block_rows: block_costs(block_rows, coarse_means), embeddings.reshape(ROWS // block_size, block_size, D))
    return coarse_update, fine_update, nearest_cost.reshape(ROWS)
```

```python
import functools

import jax
import jax.numpy as jnp
from jax import lax
from jax.experimental import pallas as pl
from jax.experimental.pallas import tpu as pltpu
from jax.sharding import PartitionSpec as P

SUB = 64
DIRECT = 32
SPILL = 128
BATCH = 16
Z_SIZE, Y_SIZE = 8, 4
VMEM_BYTES = 56 * 2**20
MESH = pl.DeviceIdType.MESH


def nt_dot(left, right):
    return lax.dot_general(left, right, (((1,), (1,)), ((), ())), preferred_element_type=jnp.float32)


def pack_kernel(x_ref, position_ref, out_ref, turned):
    features = x_ref.shape[1]
    share = 96
    k = lax.broadcasted_iota(jnp.int32, (features, features), 0)
    within = k % share
    feature = k - within + jnp.where(within < share // 2, 2 * within, 2 * within - share + 1)
    select = feature == lax.broadcasted_iota(jnp.int32, (features, features), 1)
    select = jnp.where(select, 1.0, 0.0).astype(jnp.bfloat16)
    turned[...] = nt_dot(select, x_ref[...]).astype(jnp.bfloat16)
    positions = position_ref[...]
    for tile in range(out_ref.shape[1] // 128):
        ids = tile * 128 + lax.broadcasted_iota(jnp.int32, (128, positions.shape[1]), 0)
        hits = jnp.where(positions == ids, 1.0, 0.0).astype(jnp.bfloat16)
        out_ref[:, tile * 128 : (tile + 1) * 128] = nt_dot(turned[...], hits).astype(jnp.bfloat16)


def pack(embeddings, position, width):
    rows, features = embeddings.shape
    return pl.pallas_call(
        pack_kernel,
        out_shape=jax.ShapeDtypeStruct((features, width), jnp.bfloat16),
        scratch_shapes=[pltpu.VMEM((features, rows), jnp.bfloat16)],
        compiler_params=pltpu.CompilerParams(vmem_limit_bytes=VMEM_BYTES),
    )(embeddings, position.reshape(1, rows))


def regroup_kernel(in_ref, direct_ref, spill_ref):
    members = in_ref.shape[0]
    quads = direct_ref.shape[0] // 4
    to = lax.broadcasted_iota(jnp.int32, (1024, 1024), 0)
    source = (to // DIRECT) % members * 128 + to // (DIRECT * members) * DIRECT + to % DIRECT
    move = source == lax.broadcasted_iota(jnp.int32, (1024, 1024), 1)
    move = jnp.where(move, 1.0, 0.0).astype(jnp.bfloat16)
    for quad in range(quads):
        block = jnp.concatenate(
            [in_ref[m, :, quad * 128 : (quad + 1) * 128] for m in range(members)], axis=1
        )
        moved = nt_dot(block, move).astype(jnp.bfloat16)
        for i in range(4):
            direct_ref[quad * 4 + i] = moved[:, i * 256 : (i + 1) * 256]
    for m in range(members):
        spill_ref[:, m * SPILL : (m + 1) * SPILL] = in_ref[m, :, quads * 128 :]


def regroup(arrived, owners):
    members, share, _ = arrived.shape
    return pl.pallas_call(
        regroup_kernel,
        out_shape=(
            jax.ShapeDtypeStruct((owners, share, members * DIRECT), jnp.bfloat16),
            jax.ShapeDtypeStruct((share, members * SPILL), jnp.bfloat16),
        ),
        compiler_params=pltpu.CompilerParams(vmem_limit_bytes=VMEM_BYTES),
    )(arrived)


def spread_kernel(block_ref, out_ref, send_sem, recv_sem, local_sem):
    me = lax.axis_index("dp")
    z, y = me // Y_SIZE, me % Y_SIZE

    def owner(z_at, y_at):
        return lax.rem(z_at + Z_SIZE, Z_SIZE) * Y_SIZE + lax.rem(y_at + Y_SIZE, Y_SIZE)

    sides = {"y": (owner(z, y + 1), owner(z, y - 1)), "z": (owner(z + 1, y), owner(z - 1, y))}
    barrier = pltpu.get_barrier_semaphore()
    for axis in "yz":
        for side in sides[axis]:
            pl.semaphore_signal(barrier, inc=1, device_id={"dp": side}, device_id_type=MESH)
    pl.semaphore_wait(barrier, 4)
    own = pltpu.make_async_copy(block_ref, out_ref.at[z, y], local_sem)
    own.start()
    half_rows, width = block_ref.shape[0] // 2, block_ref.shape[1]
    copies = {}
    count = [0]

    def begin(half, axis, step, first):
        size = Y_SIZE if axis == "y" else Z_SIZE
        last = step == size // 2
        for side in range(2):
            back = (step - 1) * (1 if side == 0 else -1)
            lanes = pl.ds(0, width)
            if last:
                lanes = pl.ds(side * width // 2, width // 2)
            rows = pl.ds(half * half_rows, half_rows)
            at_z = lax.rem(z - back + Z_SIZE, Z_SIZE) if axis == "z" else z
            at_y = lax.rem(y - back + Y_SIZE, Y_SIZE) if axis == "y" else y
            if first:
                place = out_ref.at[at_z, at_y, rows, lanes]
                source = block_ref.at[rows, lanes] if step == 1 else place
            else:
                if axis == "z":
                    place = out_ref.at[at_z, :, rows, lanes]
                else:
                    place = out_ref.at[:, at_y, rows, lanes]
                source = place
            index = count[0]
            count[0] += 1
            copy = pltpu.make_async_remote_copy(
                src_ref=source,
                dst_ref=place,
                send_sem=send_sem.at[index],
                recv_sem=recv_sem.at[index],
                device_id={"dp": sides[axis][side]},
                device_id_type=MESH,
            )
            copy.start()
            copies[(half, axis, step, side)] = copy

    def arrive(half, axis, step):
        for side in range(2):
            copies[(half, axis, step, side)].wait_recv()

    begin(0, "y", 1, True)
    begin(1, "z", 1, True)
    own.wait()
    arrive(0, "y", 1)
    begin(0, "y", 2, True)
    arrive(1, "z", 1)
    begin(1, "z", 2, True)
    arrive(0, "y", 2)
    begin(0, "z", 1, False)
    for step in (2, 3):
        arrive(1, "z", step)
        begin(1, "z", step + 1, True)
    arrive(1, "z", 4)
    begin(1, "y", 1, False)
    for step in (1, 2):
        arrive(0, "z", step)
        begin(0, "z", step + 1, False)
    arrive(1, "y", 1)
    begin(1, "y", 2, False)
    arrive(0, "z", 3)
    begin(0, "z", 4, False)
    arrive(1, "y", 2)
    arrive(0, "z", 4)
    for copy in copies.values():
        copy.wait_send()


def spread(block):
    return pl.pallas_call(
        spread_kernel,
        in_specs=[pl.BlockSpec(memory_space=pl.ANY)],
        out_specs=pl.BlockSpec(memory_space=pl.ANY),
        out_shape=jax.ShapeDtypeStruct((Z_SIZE, Y_SIZE) + block.shape, block.dtype),
        scratch_shapes=[
            pltpu.SemaphoreType.DMA((24,)),
            pltpu.SemaphoreType.DMA((24,)),
            pltpu.SemaphoreType.DMA,
        ],
        compiler_params=pltpu.CompilerParams(collective_id=0, has_side_effects=True),
        cost_estimate=pl.CostEstimate(flops=0, bytes_accessed=2**24, transcendentals=0),
    )(block)


def scatter_kernel(direct_steps, tags, tag_row_ref, direct_ref, spill_ref, cells_ref, sums_ref, combined):
    step = pl.program_id(0)

    @pl.when(step == 0)
    def _():
        cells_ref[...] = jnp.zeros_like(cells_ref)

    batch_of = lambda dim: lax.broadcasted_iota(jnp.int32, (128, 128), dim) // BATCH
    near = batch_of(0) == batch_of(1)

    def combine(block, values):
        tag = jnp.broadcast_to(tag_row_ref[0, :, block * 128 : (block + 1) * 128], (128, 128))
        same = (tag == tag.T) & near
        same = jnp.where(same, 1.0, 0.0).astype(jnp.bfloat16)
        ones = jnp.ones((32, 128), jnp.bfloat16)
        combined[block * 128 : (block + 1) * 128, :] = nt_dot(
            same, jnp.concatenate([values, ones], axis=0)
        )

    @pl.when(step < direct_steps)
    def _():
        for block in range(8):
            combine(block, direct_ref[block // 2, :, block % 2 * 128 : (block % 2 + 1) * 128])

    @pl.when(step >= direct_steps)
    def _():
        for block in range(8):
            combine(block, spill_ref[0, :, block * 128 : (block + 1) * 128])

    def add_batch(batch, carry):
        at = [tags[0, 0, batch * BATCH + u] for u in range(BATCH)]
        fresh = [
            cells_ref[pl.ds(at[u], 1), :] + combined[pl.ds(batch * BATCH + u, 1), :]
            for u in range(BATCH)
        ]
        for u in range(BATCH):
            cells_ref[pl.ds(at[u], 1), :] = fresh[u]
        return carry

    lax.fori_loop(0, 1024 // BATCH, add_batch, 0)

    @pl.when(step == pl.num_programs(0) - 1)
    def _():
        def slot_sums(group, carry):
            for u in range(8):
                rows = cells_ref[pl.ds((group * 8 + u) * SUB, SUB), :]
                sums_ref[pl.ds(group * 8 + u, 1), :] = jnp.sum(rows, axis=0, keepdims=True)
            return carry

        lax.fori_loop(0, sums_ref.shape[0] // 8, slot_sums, 0)


def scatter(tags, direct, spilled, slots):
    direct_steps = direct.shape[0] // 4
    spill_steps = spilled.shape[0]
    share = direct.shape[1]
    steps = direct_steps + spill_steps
    return pl.pallas_call(
        functools.partial(scatter_kernel, direct_steps),
        grid=(steps,),
        in_specs=[
            pl.BlockSpec((1, 1, 1024), lambda i: (i, 0, 0), memory_space=pltpu.SMEM),
            pl.BlockSpec((1, 1, 1024), lambda i: (i, 0, 0)),
            pl.BlockSpec((4, share, 256), lambda i: (jnp.minimum(i, direct_steps - 1), 0, 0)),
            pl.BlockSpec((1, share, 1024), lambda i: (jnp.maximum(i - direct_steps, 0), 0, 0)),
        ],
        out_specs=(
            pl.BlockSpec((slots * SUB + 8, 128), lambda i: (0, 0)),
            pl.BlockSpec((slots, 128), lambda i: (0, 0)),
        ),
        out_shape=(
            jax.ShapeDtypeStruct((slots * SUB + 8, 128), jnp.float32),
            jax.ShapeDtypeStruct((slots, 128), jnp.float32),
        ),
        scratch_shapes=[pltpu.VMEM((1024, 128), jnp.float32)],
        compiler_params=pltpu.CompilerParams(vmem_limit_bytes=VMEM_BYTES),
    )(tags, tags, direct, spilled)


def update_kernel(cells_ref, old_ref, out_ref, turned, counts):
    first = lax.broadcasted_iota(jnp.int32, (48, 128), 1) < SUB
    first_row = first[0:1]
    for pair in range(8):
        block = cells_ref[pair * 128 : (pair + 1) * 128, :].T
        rolled = pltpu.roll(block, SUB, 1)
        even = jnp.where(first, block[0:48], rolled[48:96])
        odd = jnp.where(first, rolled[0:48], block[48:96])
        slot = 2 * pair
        turned[slot // 8, pl.ds(slot % 8, 48, stride=8), :] = even
        turned[slot // 8, pl.ds(slot % 8 + 1, 48, stride=8), :] = odd
        counts[slot : slot + 1, :] = jnp.where(first_row, block[96:97], rolled[96:97])
        counts[slot + 1 : slot + 2, :] = jnp.where(first_row, rolled[96:97], block[96:97])
    scale = 1.0 / (counts[...] + 1.0)
    for tile in range(48):
        sums = jnp.concatenate(
            [turned[0, tile * 8 : (tile + 1) * 8, :], turned[1, tile * 8 : (tile + 1) * 8, :]], axis=0
        )
        old = old_ref[:, tile * 128 : (tile + 1) * 128].astype(jnp.float32)
        out_ref[:, tile * 128 : (tile + 1) * 128] = ((sums + old) * scale).astype(jnp.bfloat16)


def update(cells, fine_means):
    slots, width = fine_means.shape
    return pl.pallas_call(
        update_kernel,
        grid=(slots // 16,),
        in_specs=[
            pl.BlockSpec((16 * SUB, 128), lambda i: (i, 0)),
            pl.BlockSpec((16, width), lambda i: (i, 0)),
        ],
        out_specs=pl.BlockSpec((16, width), lambda i: (i, 0)),
        out_shape=jax.ShapeDtypeStruct((slots, width), jnp.bfloat16),
        scratch_shapes=[pltpu.VMEM((2, 48 * 8, 128), jnp.float32), pltpu.VMEM((16, 128), jnp.float32)],
        compiler_params=pltpu.CompilerParams(vmem_limit_bytes=VMEM_BYTES),
        cost_estimate=pl.CostEstimate(flops=2**24, bytes_accessed=2**24, transcendentals=0),
    )(cells, fine_means)


def lowest_kernel(x_ref, centroids_ref, out_ref, doubled, lowest):
    step = pl.program_id(0)

    @pl.when(step == 0)
    def _():
        doubled[...] = x_ref[...] * jnp.bfloat16(-2.0)
        lowest[...] = jnp.full_like(lowest, jnp.inf)

    for part in range(centroids_ref.shape[0] // 256):
        piece = centroids_ref[part * 256 : (part + 1) * 256, :]
        wide = piece.astype(jnp.float32)
        norms = jnp.sum(wide * wide, axis=1, keepdims=True)
        costs = nt_dot(piece, doubled[...]) + norms
        costs = jnp.min(costs.reshape(32, 8, costs.shape[1]), axis=0)
        lowest[...] = jnp.minimum(lowest[...], costs)

    @pl.when(step == pl.num_programs(0) - 1)
    def _():
        out_ref[...] = jnp.min(lowest[...], axis=0, keepdims=True)


def lowest_cost(embeddings, centroids):
    rows, features = embeddings.shape
    total = centroids.shape[0]
    return pl.pallas_call(
        lowest_kernel,
        grid=(total // 1024,),
        in_specs=[
            pl.BlockSpec((rows, features), lambda i: (0, 0)),
            pl.BlockSpec((1024, features), lambda i: (i, 0)),
        ],
        out_specs=pl.BlockSpec((1, rows), lambda i: (0, 0)),
        out_shape=jax.ShapeDtypeStruct((1, rows), jnp.float32),
        scratch_shapes=[pltpu.VMEM((rows, features), jnp.bfloat16), pltpu.VMEM((8, rows), jnp.float32)],
        compiler_params=pltpu.CompilerParams(vmem_limit_bytes=VMEM_BYTES),
        cost_estimate=pl.CostEstimate(
            flops=2 * rows * features * total, bytes_accessed=2 * features * total, transcendentals=0
        ),
    )(embeddings, centroids)[0]


def on_device(embeddings, coarse_label, fine_label, slot_table, coarse_means, fine_means):
    row_count, feature_count = embeddings.shape
    owner_count = lax.axis_size("dp")
    member_count = lax.axis_size("group")
    slots = fine_means.shape[0]
    share = feature_count // member_count
    table_cells = slots * SUB
    me = lax.axis_index("dp")

    centroids = lax.all_gather(coarse_means, ("dp", "group"), axis=0, tiled=True)

    slot_index = jnp.take(slot_table, coarse_label)
    owner_index = slot_index // slots
    matches = owner_index[:, None] == jnp.arange(owner_count, dtype=jnp.int32)[None, :]
    row_ids = jnp.arange(row_count, dtype=jnp.int32)
    before = (row_ids[:, None] > row_ids[None, :]).astype(jnp.bfloat16)
    earlier = jnp.dot(before, matches.astype(jnp.bfloat16), preferred_element_type=jnp.float32)
    excess = jnp.maximum(jnp.sum(matches.astype(jnp.int32), axis=0) - DIRECT, 0)
    offsets = jnp.cumsum(excess) - excess
    excess_total = jnp.sum(excess)
    rank = jnp.sum(jnp.where(matches, earlier, 0.0), axis=1).astype(jnp.int32)
    offset = jnp.sum(jnp.where(matches, offsets[None, :], 0), axis=1)
    direct_width = owner_count * DIRECT
    position = jnp.where(
        rank < DIRECT, owner_index * DIRECT + rank, direct_width + offset + rank - DIRECT
    )
    cell = slot_index * SUB + fine_label
    width = direct_width + SPILL

    def tags_at(position_ids):
        hits = position[None, :] == position_ids[:, None]
        return jnp.sum(jnp.where(hits, cell[None, :] + 1, 0), axis=1)

    position_ids = jnp.arange(width + 128, dtype=jnp.int32)
    tags = jnp.where(
        position_ids < width,
        tags_at(jnp.where(position_ids < width, position_ids, -1)),
        excess_total,
    )
    all_tags = lax.all_gather(tags, ("dp", "group"), axis=0, tiled=False)

    packed = pack(embeddings, position, width).reshape(member_count, share, width)
    arrived = lax.all_to_all(packed, "group", split_axis=0, concat_axis=0, tiled=True)
    direct, spill = regroup(arrived, owner_count)
    direct = lax.all_to_all(direct, "dp", split_axis=0, concat_axis=0, tiled=True)
    spilled = spread(spill).reshape(owner_count, share, member_count * SPILL)

    def local_cells(global_tags):
        local = global_tags - 1 - me * table_cells
        return jnp.where((local >= 0) & (local < table_cells), local, table_cells)

    direct_tags = lax.dynamic_slice_in_dim(all_tags, me * DIRECT, DIRECT, axis=1)
    spill_tags = all_tags[:, direct_width:width]
    step_tags = jnp.concatenate(
        [direct_tags.reshape(-1, 1, 1024), spill_tags.reshape(-1, 1, 1024)], axis=0
    )
    cells, sums = scatter(local_cells(step_tags), direct, spilled, slots)
    rounds = (jnp.max(all_tags[:, width]) + SPILL - 1) // SPILL

    def more(state):
        return state[0] < rounds

    def another_round(state):
        number, cells, sums = state
        ids = direct_width + number * SPILL + jnp.arange(SPILL, dtype=jnp.int32)
        hits = (position[None, :] == ids[:, None]).astype(jnp.bfloat16)
        rows = jnp.dot(hits, embeddings, preferred_element_type=jnp.float32).astype(jnp.bfloat16)
        rows = rows.reshape(SPILL, member_count, share // 2, 2).transpose(1, 0, 3, 2)
        rows = rows.reshape(member_count, SPILL, share)
        rows = lax.all_to_all(rows, "group", split_axis=0, concat_axis=0, tiled=True)
        rows = lax.all_gather(rows, "dp", axis=0, tiled=True).reshape(-1, share)
        round_cells = lax.all_gather(tags_at(ids), ("dp", "group"), axis=0, tiled=True)
        round_cells = local_cells(round_cells)
        ones = jnp.ones((rows.shape[0], 128 - share), jnp.float32)
        rows = jnp.concatenate([rows.astype(jnp.float32), ones], axis=1)
        cells = cells.at[round_cells].add(rows)
        sums = sums + jax.ops.segment_sum(rows, round_cells // SUB, num_segments=slots + 1)[:slots]
        return number + 1, cells, sums

    _, cells, sums = lax.while_loop(more, another_round, (jnp.int32(1), cells, sums))

    own = lax.all_to_all(
        sums.reshape(member_count, -1, 128), "group", split_axis=0, concat_axis=0, tiled=True
    )
    fine_update = update(cells, fine_means)
    own_count = own[0, :, share]
    own_sums = own[:, :, :share].reshape(member_count, -1, 2, share // 2)
    own_sums = own_sums.transpose(1, 0, 3, 2).reshape(-1, feature_count)
    coarse_update = (
        (own_sums + coarse_means.astype(jnp.float32)) / (own_count[:, None] + 1.0)
    ).astype(jnp.bfloat16)

    own_norms = jnp.sum(jnp.square(embeddings.astype(jnp.float32)), axis=1)
    nearest_cost = (own_norms + lowest_cost(embeddings, centroids)) / feature_count
    return (coarse_update, fine_update, nearest_cost)


def solution(mesh):
    placed = (
        P(("dp", "group"), None),
        P(("dp", "group")),
        P(("dp", "group")),
        P(),
        P(("dp", "group"), None),
        P("dp", "group"),
    )
    return jax.shard_map(
        on_device,
        mesh=mesh,
        in_specs=placed,
        out_specs=(P(("dp", "group"), None), P("dp", "group"), P(("dp", "group"))),
        check_vma=False,
    )
```

```python
import functools

import jax
import jax.numpy as jnp
from jax import lax
from jax.experimental import pallas as pl
from jax.experimental.pallas import tpu as pltpu
from jax.sharding import PartitionSpec as P

SUB = 64
DIRECT = 32
SPILL = 128
BATCH = 8
Z_SIZE, Y_SIZE = 8, 4
VMEM_BYTES = 56 * 2**20
MESH = pl.DeviceIdType.MESH


def nt_dot(left, right):
    return lax.dot_general(left, right, (((1,), (1,)), ((), ())), preferred_element_type=jnp.float32)


def pack_kernel(x_ref, position_ref, out_ref, turned):
    features = x_ref.shape[1]
    share = 96
    k = lax.broadcasted_iota(jnp.int32, (features, features), 0)
    within = k % share
    feature = k - within + jnp.where(within < share // 2, 2 * within, 2 * within - share + 1)
    select = feature == lax.broadcasted_iota(jnp.int32, (features, features), 1)
    select = jnp.where(select, 1.0, 0.0).astype(jnp.bfloat16)
    turned[...] = nt_dot(select, x_ref[...]).astype(jnp.bfloat16)
    positions = position_ref[...]
    for tile in range(out_ref.shape[1] // 128):
        ids = tile * 128 + lax.broadcasted_iota(jnp.int32, (128, positions.shape[1]), 0)
        hits = jnp.where(positions == ids, 1.0, 0.0).astype(jnp.bfloat16)
        out_ref[:, tile * 128 : (tile + 1) * 128] = nt_dot(turned[...], hits).astype(jnp.bfloat16)


def pack(embeddings, position, width):
    rows, features = embeddings.shape
    return pl.pallas_call(
        pack_kernel,
        out_shape=jax.ShapeDtypeStruct((features, width), jnp.bfloat16),
        scratch_shapes=[pltpu.VMEM((features, rows), jnp.bfloat16)],
        compiler_params=pltpu.CompilerParams(vmem_limit_bytes=VMEM_BYTES),
    )(embeddings, position.reshape(1, rows))


def regroup_kernel(in_ref, direct_ref, spill_ref):
    members = in_ref.shape[0]
    quads = direct_ref.shape[0] // 4
    to = lax.broadcasted_iota(jnp.int32, (512, 512), 0)
    source = (to // DIRECT) % 4 * 128 + to // 128 * DIRECT + to % DIRECT
    move = source == lax.broadcasted_iota(jnp.int32, (512, 512), 1)
    move = jnp.where(move, 1.0, 0.0).astype(jnp.bfloat16)
    for half in range(members // 4):
        for quad in range(quads):
            block = jnp.concatenate(
                [in_ref[half * 4 + m, :, quad * 128 : (quad + 1) * 128] for m in range(4)], axis=1
            )
            moved = nt_dot(block, move).astype(jnp.bfloat16)
            for i in range(4):
                direct_ref[quad * 4 + i, :, half * 128 : (half + 1) * 128] = moved[
                    :, i * 128 : (i + 1) * 128
                ]
    for m in range(members):
        spill_ref[:, m * SPILL : (m + 1) * SPILL] = in_ref[m, :, quads * 128 :]


def regroup(arrived, owners):
    members, share, _ = arrived.shape
    return pl.pallas_call(
        regroup_kernel,
        out_shape=(
            jax.ShapeDtypeStruct((owners, share, members * DIRECT), jnp.bfloat16),
            jax.ShapeDtypeStruct((share, members * SPILL), jnp.bfloat16),
        ),
        compiler_params=pltpu.CompilerParams(vmem_limit_bytes=VMEM_BYTES),
    )(arrived)


class Rings:
    def __init__(self, planes, send_sem, recv_sem):
        me = lax.axis_index("dp")
        self.z, self.y = me // Y_SIZE, me % Y_SIZE
        self.planes, self.send_sem, self.recv_sem = planes, send_sem, recv_sem
        self.copies, self.count = {}, 0
        z, y = self.z, self.y
        self.sides = {
            "y": (self.owner(z, y + 1), self.owner(z, y - 1)),
            "z": (self.owner(z + 1, y), self.owner(z - 1, y)),
        }

    @staticmethod
    def owner(z_at, y_at):
        return lax.rem(z_at + Z_SIZE, Z_SIZE) * Y_SIZE + lax.rem(y_at + Y_SIZE, Y_SIZE)

    def greet(self):
        barrier = pltpu.get_barrier_semaphore()
        for axis in "yz":
            for side in self.sides[axis]:
                pl.semaphore_signal(barrier, inc=1, device_id={"dp": side}, device_id_type=MESH)

    def at(self, axis, first, back):
        at_z = lax.rem(self.z - back + Z_SIZE, Z_SIZE) if axis == "z" else self.z
        at_y = lax.rem(self.y - back + Y_SIZE, Y_SIZE) if axis == "y" else self.y
        if first:
            return (at_z, at_y)
        return (at_z, slice(None)) if axis == "z" else (slice(None), at_y)

    def send(self, key, source, place, device):
        copy = pltpu.make_async_remote_copy(
            src_ref=source,
            dst_ref=place,
            send_sem=self.send_sem.at[self.count],
            recv_sem=self.recv_sem.at[self.count],
            device_id=device,
            device_id_type=MESH,
        )
        self.count += 1
        copy.start()
        self.copies.setdefault(key, []).append(copy)

    def begin(self, half, axis, step):
        first = (axis == "y") == (half == 0)
        last = step == (Y_SIZE if axis == "y" else Z_SIZE) // 2
        for side in range(2):
            at = self.at(axis, first, (step - 1) * (1 if side == 0 else -1))
            for own, everyone, half_index, side_index in self.planes:
                index = half_index(half)
                if last:
                    index = side_index(side, index)
                place = everyone.at[at + index]
                source = own.at[index] if first and step == 1 and own is not None else place
                self.send((half, axis, step), source, place, {"dp": self.sides[axis][side]})

    def arrive(self, *key):
        for copy in self.copies[key]:
            copy.wait_recv()

    def run(self, arrived=lambda *key: None):
        def arrive(*key):
            self.arrive(*key)
            arrived(*key)

        self.begin(0, "y", 1)
        self.begin(1, "z", 1)
        self.arrive(0, "y", 1)
        self.begin(0, "y", 2)
        self.arrive(1, "z", 1)
        self.begin(1, "z", 2)
        self.arrive(0, "y", 2)
        self.begin(0, "z", 1)
        arrived(0, "y", 2)
        for step in (2, 3):
            self.arrive(1, "z", step)
            self.begin(1, "z", step + 1)
        self.arrive(1, "z", 4)
        self.begin(1, "y", 1)
        arrived(1, "z", 4)
        for step in (1, 2):
            self.arrive(0, "z", step)
            self.begin(0, "z", step + 1)
            arrived(0, "z", step)
        self.arrive(1, "y", 1)
        self.begin(1, "y", 2)
        arrived(1, "y", 1)
        self.arrive(0, "z", 3)
        self.begin(0, "z", 4)
        arrived(0, "z", 3)
        arrive(1, "y", 2)
        arrive(0, "z", 4)

    def finish(self):
        for group in self.copies.values():
            for copy in group:
                copy.wait_send()


def spread_kernel(block_ref, out_ref, send_sem, recv_sem, local_sem):
    width = block_ref.shape[1]
    halves = (pl.ds(0, 32), pl.ds(32, 64))
    plane = (
        block_ref,
        out_ref,
        lambda half: (halves[half], pl.ds(0, width)),
        lambda side, index: (index[0], pl.ds(side * width // 2, width // 2)),
    )
    rings = Rings([plane], send_sem, recv_sem)
    rings.greet()
    pl.semaphore_wait(pltpu.get_barrier_semaphore(), 4)
    own = pltpu.make_async_copy(block_ref, out_ref.at[rings.z, rings.y], local_sem)
    own.start()
    own.wait()
    rings.run()
    rings.finish()


def spread(block):
    return pl.pallas_call(
        spread_kernel,
        in_specs=[pl.BlockSpec(memory_space=pl.ANY)],
        out_specs=pl.BlockSpec(memory_space=pl.ANY),
        out_shape=jax.ShapeDtypeStruct((Z_SIZE, Y_SIZE) + block.shape, block.dtype),
        scratch_shapes=[
            pltpu.SemaphoreType.DMA((24,)),
            pltpu.SemaphoreType.DMA((24,)),
            pltpu.SemaphoreType.DMA,
        ],
        compiler_params=pltpu.CompilerParams(collective_id=0, has_side_effects=True),
        cost_estimate=pl.CostEstimate(flops=0, bytes_accessed=2**24, transcendentals=0),
    )(block)


def share_kernel(means_ref, tags_ref, all_means, all_tags, send_sem, recv_sem, local_sem):
    member = lax.axis_index("group")
    x, core = member // 2, member % 2
    means, tags = all_means.at[core], all_tags.at[core]

    def plane(everyone, rows):
        return (
            None,
            everyone,
            lambda half: (slice(None), pl.ds(half * rows, rows)),
            lambda side, index: (pl.ds(side * 2, 2), index[1]),
        )

    planes = [plane(means, 16), plane(tags, 8)]
    rings = Rings(planes, send_sem, recv_sem)
    sibling = {"group": x * 2 + 1 - core}
    others = [{"group": lax.rem(x + step, 4) * 2 + core} for step in (1, 2, 3)]
    barrier = pltpu.get_barrier_semaphore()
    rings.greet()
    for other in others + [sibling]:
        pl.semaphore_signal(barrier, inc=1, device_id=other, device_id_type=MESH)
    pl.semaphore_wait(barrier, 8)
    z, y = rings.z, rings.y
    blocks = [(means_ref, means.at[z, y, x]), (tags_ref, tags.at[z, y, x])]
    local = [pltpu.make_async_copy(*block, local_sem.at[i]) for i, block in enumerate(blocks)]
    for copy in local:
        copy.start()
    for other in others:
        for source, place in blocks:
            rings.send(("x",), source, place, other)
    for copy in local:
        copy.wait()
    rings.arrive("x")

    def to_sibling(half, axis, step):
        first = (axis == "y") == (half == 0)
        last = step == (Y_SIZE if axis == "y" else Z_SIZE) // 2
        if first:
            places = [self_at("z" if axis == "y" else "y", 0)]
        elif last:
            places = [self_at(axis, step)]
        else:
            places = [self_at(axis, step), self_at(axis, -step)]
        for at in places:
            for _, everyone, half_index, _ in planes:
                place = everyone.at[at + half_index(half)]
                rings.send(("core",), place, place, sibling)

    def self_at(axis, back):
        return rings.at(axis, False, back)

    rings.run(to_sibling)
    rings.arrive("core")
    rings.finish()


def share_all(means, tags):
    any_space = pl.BlockSpec(memory_space=pl.ANY)
    return pl.pallas_call(
        share_kernel,
        in_specs=[any_space, any_space],
        out_specs=(any_space, any_space),
        out_shape=(
            jax.ShapeDtypeStruct((2, Z_SIZE, Y_SIZE, 4) + means.shape, means.dtype),
            jax.ShapeDtypeStruct((2, Z_SIZE, Y_SIZE, 4) + tags.shape, tags.dtype),
        ),
        scratch_shapes=[
            pltpu.SemaphoreType.DMA((80,)),
            pltpu.SemaphoreType.DMA((80,)),
            pltpu.SemaphoreType.DMA((2,)),
        ],
        compiler_params=pltpu.CompilerParams(collective_id=1, has_side_effects=True),
        cost_estimate=pl.CostEstimate(flops=0, bytes_accessed=2**24, transcendentals=0),
    )(means, tags)


def scatter_kernel(direct_steps, tags, tag_row_ref, direct_ref, spill_ref, cells_ref, sums_ref, other, combined):
    step = pl.program_id(0)
    tables = (cells_ref, other)

    @pl.when(step == 0)
    def _():
        for table in tables:
            table[...] = jnp.zeros_like(table)

    def add_rows(values):
        batch_of = lambda dim: lax.broadcasted_iota(jnp.int32, (128, 128), dim) // BATCH
        near = batch_of(0) == batch_of(1)
        ones = jnp.ones((32, 128), jnp.bfloat16)
        for block in range(8):
            tag = jnp.broadcast_to(tag_row_ref[0, :, block * 128 : (block + 1) * 128], (128, 128))
            same = jnp.where((tag == tag.T) & near, 1.0, 0.0).astype(jnp.bfloat16)
            combined[block * 128 : (block + 1) * 128, :] = nt_dot(
                same, jnp.concatenate([values(block), ones], axis=0)
            )
        held = None
        for batch in range(1024 // BATCH + 1):
            fresh = []
            for u in range(BATCH):
                if batch < 1024 // BATCH:
                    row = batch * BATCH + u
                    at = tags[0, 0, row]
                    sums = tables[batch % 2][pl.ds(at, 1), :] + combined[row : row + 1, :]
                    fresh.append((at, sums))
                if held is not None:
                    tables[1 - batch % 2][pl.ds(held[u][0], 1), :] = held[u][1]
            held = fresh

    @pl.when(step < direct_steps)
    def _():
        add_rows(lambda block: direct_ref[block // 2, :, block % 2 * 128 : (block % 2 + 1) * 128])

    @pl.when(step >= direct_steps)
    def _():
        add_rows(lambda block: spill_ref[0, :, block * 128 : (block + 1) * 128])

    @pl.when(step == pl.num_programs(0) - 1)
    def _():
        def slot_sums(group, carry):
            for u in range(8):
                at = pl.ds(pl.multiple_of((group * 8 + u) * SUB, SUB), SUB)
                rows = cells_ref[at, :] + other[at, :]
                cells_ref[at, :] = rows
                sums_ref[pl.ds(group * 8 + u, 1), :] = jnp.sum(rows, axis=0, keepdims=True)
            return carry

        lax.fori_loop(0, sums_ref.shape[0] // 8, slot_sums, 0)


def scatter(tags, direct, spilled, slots):
    direct_steps = direct.shape[0] // 4
    spill_steps = spilled.shape[0]
    share = direct.shape[1]
    return pl.pallas_call(
        functools.partial(scatter_kernel, direct_steps),
        grid=(direct_steps + spill_steps,),
        in_specs=[
            pl.BlockSpec((1, 1, 1024), lambda i: (i, 0, 0), memory_space=pltpu.SMEM),
            pl.BlockSpec((1, 1, 1024), lambda i: (i, 0, 0)),
            pl.BlockSpec((4, share, 256), lambda i: (jnp.minimum(i, direct_steps - 1), 0, 0)),
            pl.BlockSpec((1, share, 1024), lambda i: (jnp.maximum(i - direct_steps, 0), 0, 0)),
        ],
        out_specs=(
            pl.BlockSpec((slots * SUB + 8, 128), lambda i: (0, 0)),
            pl.BlockSpec((slots, 128), lambda i: (0, 0)),
        ),
        out_shape=(
            jax.ShapeDtypeStruct((slots * SUB + 8, 128), jnp.float32),
            jax.ShapeDtypeStruct((slots, 128), jnp.float32),
        ),
        scratch_shapes=[
            pltpu.VMEM((slots * SUB + 8, 128), jnp.float32),
            pltpu.VMEM((1024, 128), jnp.float32),
        ],
        compiler_params=pltpu.CompilerParams(vmem_limit_bytes=VMEM_BYTES),
    )(tags, tags, direct, spilled)


def update_kernel(cells_ref, old_ref, out_ref, turned, counts):
    first = lax.broadcasted_iota(jnp.int32, (48, 128), 1) < SUB
    first_row = first[0:1]
    for pair in range(8):
        block = cells_ref[pair * 128 : (pair + 1) * 128, :].T
        rolled = pltpu.roll(block, SUB, 1)
        even = jnp.where(first, block[0:48], rolled[48:96])
        odd = jnp.where(first, rolled[0:48], block[48:96])
        slot = 2 * pair
        turned[slot // 8, pl.ds(slot % 8, 48, stride=8), :] = even
        turned[slot // 8, pl.ds(slot % 8 + 1, 48, stride=8), :] = odd
        counts[slot : slot + 1, :] = jnp.where(first_row, block[96:97], rolled[96:97])
        counts[slot + 1 : slot + 2, :] = jnp.where(first_row, rolled[96:97], block[96:97])
    scale = 1.0 / (counts[...] + 1.0)
    for tile in range(48):
        sums = jnp.concatenate(
            [turned[0, tile * 8 : (tile + 1) * 8, :], turned[1, tile * 8 : (tile + 1) * 8, :]], axis=0
        )
        old = old_ref[:, tile * 128 : (tile + 1) * 128].astype(jnp.float32)
        out_ref[:, tile * 128 : (tile + 1) * 128] = ((sums + old) * scale).astype(jnp.bfloat16)


def update(cells, fine_means):
    slots, width = fine_means.shape
    return pl.pallas_call(
        update_kernel,
        grid=(slots // 16,),
        in_specs=[
            pl.BlockSpec((16 * SUB, 128), lambda i: (i, 0)),
            pl.BlockSpec((16, width), lambda i: (i, 0)),
        ],
        out_specs=pl.BlockSpec((16, width), lambda i: (i, 0)),
        out_shape=jax.ShapeDtypeStruct((slots, width), jnp.bfloat16),
        scratch_shapes=[pltpu.VMEM((2, 48 * 8, 128), jnp.float32), pltpu.VMEM((16, 128), jnp.float32)],
        compiler_params=pltpu.CompilerParams(vmem_limit_bytes=VMEM_BYTES),
        cost_estimate=pl.CostEstimate(flops=2**24, bytes_accessed=2**24, transcendentals=0),
    )(cells, fine_means)


def lowest_kernel(x_ref, centroids_ref, out_ref, doubled, lowest):
    step = pl.program_id(0)

    @pl.when(step == 0)
    def _():
        doubled[...] = x_ref[...] * jnp.bfloat16(-2.0)
        lowest[...] = jnp.full_like(lowest, jnp.inf)

    for part in range(centroids_ref.shape[0] // 256):
        piece = centroids_ref[part * 256 : (part + 1) * 256, :]
        wide = piece.astype(jnp.float32)
        norms = jnp.sum(wide * wide, axis=1, keepdims=True)
        costs = nt_dot(piece, doubled[...]) + norms
        costs = jnp.min(costs.reshape(32, 8, costs.shape[1]), axis=0)
        lowest[...] = jnp.minimum(lowest[...], costs)

    @pl.when(step == pl.num_programs(0) - 1)
    def _():
        out_ref[...] = jnp.min(lowest[...], axis=0, keepdims=True)


def lowest_cost(embeddings, centroids):
    rows, features = embeddings.shape
    total = centroids.shape[0]
    return pl.pallas_call(
        lowest_kernel,
        grid=(total // 1024,),
        in_specs=[
            pl.BlockSpec((rows, features), lambda i: (0, 0)),
            pl.BlockSpec((1024, features), lambda i: (i, 0)),
        ],
        out_specs=pl.BlockSpec((1, rows), lambda i: (0, 0)),
        out_shape=jax.ShapeDtypeStruct((1, rows), jnp.float32),
        scratch_shapes=[pltpu.VMEM((rows, features), jnp.bfloat16), pltpu.VMEM((8, rows), jnp.float32)],
        compiler_params=pltpu.CompilerParams(vmem_limit_bytes=VMEM_BYTES),
        cost_estimate=pl.CostEstimate(
            flops=2 * rows * features * total, bytes_accessed=2 * features * total, transcendentals=0
        ),
    )(embeddings, centroids)[0]


def on_device(embeddings, coarse_label, fine_label, slot_table, coarse_means, fine_means):
    row_count, feature_count = embeddings.shape
    owner_count = lax.axis_size("dp")
    member_count = lax.axis_size("group")
    slots = fine_means.shape[0]
    share = feature_count // member_count
    table_cells = slots * SUB
    me = lax.axis_index("dp")

    slot_index = jnp.take(slot_table, coarse_label)
    owner_index = slot_index // slots
    matches = owner_index[:, None] == jnp.arange(owner_count, dtype=jnp.int32)[None, :]
    row_ids = jnp.arange(row_count, dtype=jnp.int32)
    before = (row_ids[:, None] > row_ids[None, :]).astype(jnp.bfloat16)
    earlier = jnp.dot(before, matches.astype(jnp.bfloat16), preferred_element_type=jnp.float32)
    excess = jnp.maximum(jnp.sum(matches.astype(jnp.int32), axis=0) - DIRECT, 0)
    offsets = jnp.cumsum(excess) - excess
    excess_total = jnp.sum(excess)
    rank = jnp.sum(jnp.where(matches, earlier, 0.0), axis=1).astype(jnp.int32)
    offset = jnp.sum(jnp.where(matches, offsets[None, :], 0), axis=1)
    direct_width = owner_count * DIRECT
    position = jnp.where(
        rank < DIRECT, owner_index * DIRECT + rank, direct_width + offset + rank - DIRECT
    )
    cell = slot_index * SUB + fine_label
    width = direct_width + SPILL

    def tags_at(position_ids):
        hits = position[None, :] == position_ids[:, None]
        return jnp.sum(jnp.where(hits, cell[None, :] + 1, 0), axis=1)

    tags = jnp.concatenate(
        [
            tags_at(jnp.arange(width, dtype=jnp.int32)).reshape(-1, 128),
            jnp.broadcast_to(excess_total, (16 - width // 128, 128)),
        ],
        axis=0,
    )
    packed = pack(embeddings, position, width).reshape(member_count, share, width)
    packed, tags = lax.optimization_barrier((packed, tags))
    arrived = lax.all_to_all(packed, "group", split_axis=0, concat_axis=0, tiled=True)
    centroids, all_tags = share_all(coarse_means, tags)
    arrived, centroids, all_tags = lax.optimization_barrier((arrived, centroids, all_tags))
    direct, spill = regroup(arrived, owner_count)
    direct = lax.all_to_all(direct, "dp", split_axis=0, concat_axis=0, tiled=True)
    own_norms = jnp.sum(jnp.square(embeddings.astype(jnp.float32)), axis=1)
    lowest = lowest_cost(embeddings, centroids.reshape(-1, feature_count))
    nearest_cost = (own_norms + lowest) / feature_count
    nearest_cost, spill = lax.optimization_barrier((nearest_cost, spill))
    spilled = spread(spill).reshape(owner_count, share, member_count * SPILL)

    def local_cells(global_tags):
        local = global_tags - 1 - me * table_cells
        return jnp.where((local >= 0) & (local < table_cells), local, table_cells)

    all_tags = all_tags.reshape(2, owner_count, 4, 16, 128)
    per_line = 128 // DIRECT
    direct_tags = lax.dynamic_slice_in_dim(all_tags, me // per_line, 1, axis=3)
    direct_tags = lax.dynamic_slice_in_dim(direct_tags, me % per_line * DIRECT, DIRECT, axis=4)
    spill_tags = all_tags[:, :, :, direct_width // 128]
    step_tags = jnp.concatenate(
        [
            direct_tags.reshape(2, owner_count, 4, DIRECT).transpose(1, 2, 0, 3).reshape(-1, 1, 1024),
            spill_tags.transpose(1, 2, 0, 3).reshape(-1, 1, 1024),
        ],
        axis=0,
    )
    cells, sums = scatter(local_cells(step_tags), direct, spilled, slots)
    rounds = (jnp.max(all_tags[:, :, :, width // 128, 0]) + SPILL - 1) // SPILL

    def more(state):
        return state[0] < rounds

    def another_round(state):
        number, cells, sums = state
        ids = direct_width + number * SPILL + jnp.arange(SPILL, dtype=jnp.int32)
        hits = (position[None, :] == ids[:, None]).astype(jnp.bfloat16)
        rows = jnp.dot(hits, embeddings, preferred_element_type=jnp.float32).astype(jnp.bfloat16)
        rows = rows.reshape(SPILL, member_count, share // 2, 2).transpose(1, 0, 3, 2)
        rows = rows.reshape(member_count, SPILL, share)
        rows = lax.all_to_all(rows, "group", split_axis=0, concat_axis=0, tiled=True)
        rows = lax.all_gather(rows, "dp", axis=0, tiled=True).reshape(-1, share)
        round_cells = lax.all_gather(tags_at(ids), ("dp", "group"), axis=0, tiled=True)
        round_cells = local_cells(round_cells)
        ones = jnp.ones((rows.shape[0], 128 - share), jnp.float32)
        rows = jnp.concatenate([rows.astype(jnp.float32), ones], axis=1)
        cells = cells.at[round_cells].add(rows)
        sums = sums + jax.ops.segment_sum(rows, round_cells // SUB, num_segments=slots + 1)[:slots]
        return number + 1, cells, sums

    _, cells, sums = lax.while_loop(more, another_round, (jnp.int32(1), cells, sums))

    own = lax.all_to_all(
        sums.reshape(member_count, -1, 128), "group", split_axis=0, concat_axis=0, tiled=True
    )
    fine_update = update(cells, fine_means)
    own_count = own[0, :, share]
    own_sums = own[:, :, :share].reshape(member_count, -1, 2, share // 2)
    own_sums = own_sums.transpose(1, 0, 3, 2).reshape(-1, feature_count)
    coarse_update = (
        (own_sums + coarse_means.astype(jnp.float32)) / (own_count[:, None] + 1.0)
    ).astype(jnp.bfloat16)

    return (coarse_update, fine_update, nearest_cost)


def solution(mesh):
    placed = (
        P(("dp", "group"), None),
        P(("dp", "group")),
        P(("dp", "group")),
        P(),
        P(("dp", "group"), None),
        P("dp", "group"),
    )
    return jax.shard_map(
        on_device,
        mesh=mesh,
        in_specs=placed,
        out_specs=(P(("dp", "group"), None), P("dp", "group"), P(("dp", "group"))),
        check_vma=False,
    )
```

```python
import functools

import jax
import jax.numpy as jnp
from jax import lax
from jax.experimental import pallas as pl
from jax.experimental.pallas import tpu as pltpu
from jax.sharding import PartitionSpec as P

SUB = 64
DIRECT = 32
SPILL = 128
BATCH = 8
Z_SIZE, Y_SIZE = 8, 4
VMEM_BYTES = 56 * 2**20
MESH = pl.DeviceIdType.MESH


def nt_dot(left, right):
    return lax.dot_general(left, right, (((1,), (1,)), ((), ())), preferred_element_type=jnp.float32)


def pack_kernel(x_ref, position_ref, out_ref, turned):
    features = x_ref.shape[1]
    share = 96
    k = lax.broadcasted_iota(jnp.int32, (features, features), 0)
    within = k % share
    feature = k - within + jnp.where(within < share // 2, 2 * within, 2 * within - share + 1)
    select = feature == lax.broadcasted_iota(jnp.int32, (features, features), 1)
    select = jnp.where(select, 1.0, 0.0).astype(jnp.bfloat16)
    turned[...] = nt_dot(select, x_ref[...]).astype(jnp.bfloat16)
    positions = position_ref[...]
    for tile in range(out_ref.shape[1] // 128):
        ids = tile * 128 + lax.broadcasted_iota(jnp.int32, (128, positions.shape[1]), 0)
        hits = jnp.where(positions == ids, 1.0, 0.0).astype(jnp.bfloat16)
        out_ref[:, tile * 128 : (tile + 1) * 128] = nt_dot(turned[...], hits).astype(jnp.bfloat16)


def pack(embeddings, position, width):
    rows, features = embeddings.shape
    return pl.pallas_call(
        pack_kernel,
        out_shape=jax.ShapeDtypeStruct((features, width), jnp.bfloat16),
        scratch_shapes=[pltpu.VMEM((features, rows), jnp.bfloat16)],
        compiler_params=pltpu.CompilerParams(vmem_limit_bytes=VMEM_BYTES),
    )(embeddings, position.reshape(1, rows))


def regroup_kernel(in_ref, direct_ref, spill_ref):
    members = in_ref.shape[0]
    quads = direct_ref.shape[0] // 4
    to = lax.broadcasted_iota(jnp.int32, (512, 512), 0)
    source = (to // DIRECT) % 4 * 128 + to // 128 * DIRECT + to % DIRECT
    move = source == lax.broadcasted_iota(jnp.int32, (512, 512), 1)
    move = jnp.where(move, 1.0, 0.0).astype(jnp.bfloat16)
    for half in range(members // 4):
        for quad in range(quads):
            block = jnp.concatenate(
                [in_ref[half * 4 + m, :, quad * 128 : (quad + 1) * 128] for m in range(4)], axis=1
            )
            moved = nt_dot(block, move).astype(jnp.bfloat16)
            for i in range(4):
                direct_ref[quad * 4 + i, :, half * 128 : (half + 1) * 128] = moved[
                    :, i * 128 : (i + 1) * 128
                ]
    for m in range(members):
        spill_ref[:, m * SPILL : (m + 1) * SPILL] = in_ref[m, :, quads * 128 :]


def regroup(arrived, owners):
    members, share, _ = arrived.shape
    return pl.pallas_call(
        regroup_kernel,
        out_shape=(
            jax.ShapeDtypeStruct((owners, share, members * DIRECT), jnp.bfloat16),
            jax.ShapeDtypeStruct((share, members * SPILL), jnp.bfloat16),
        ),
        compiler_params=pltpu.CompilerParams(vmem_limit_bytes=VMEM_BYTES),
    )(arrived)


class Rings:
    RATE, LATENCY = 50e3, 2.0

    def __init__(self, planes, send_sem, recv_sem):
        me = lax.axis_index("dp")
        self.z, self.y = me // Y_SIZE, me % Y_SIZE
        self.planes, self.send_sem, self.recv_sem = planes, send_sem, recv_sem
        self.copies, self.count = {}, 0
        z, y = self.z, self.y
        self.sides = {
            "y": (self.owner(z, y + 1), self.owner(z, y - 1)),
            "z": (self.owner(z + 1, y), self.owner(z - 1, y)),
        }

    @staticmethod
    def owner(z_at, y_at):
        return lax.rem(z_at + Z_SIZE, Z_SIZE) * Y_SIZE + lax.rem(y_at + Y_SIZE, Y_SIZE)

    def greet(self):
        barrier = pltpu.get_barrier_semaphore()
        for axis in "yz":
            for side in self.sides[axis]:
                pl.semaphore_signal(barrier, inc=1, device_id={"dp": side}, device_id_type=MESH)

    def at(self, second, back, offset):
        z_shift, y_shift = (-back, offset) if second == "z" else (offset, -back)
        at_z = slice(None) if z_shift is None else lax.rem(self.z + z_shift + Z_SIZE, Z_SIZE)
        at_y = slice(None) if y_shift is None else lax.rem(self.y + y_shift + Y_SIZE, Y_SIZE)
        return (at_z, at_y)

    def send(self, key, source, place, device):
        copy = pltpu.make_async_remote_copy(
            src_ref=source,
            dst_ref=place,
            send_sem=self.send_sem.at[self.count],
            recv_sem=self.recv_sem.at[self.count],
            device_id=device,
            device_id_type=MESH,
        )
        self.count += 1
        copy.start()
        self.copies.setdefault(key, []).append(copy)

    def arrive(self, *key):
        for copy in self.copies[key]:
            copy.wait_recv()

    def jobs(self):
        jobs = {}
        for plane, (_, _, _, _, sizes, eager) in enumerate(self.planes):
            for half in range(2):
                axes = "yz" if half == 0 else "zy"
                lengths = [Y_SIZE if axis == "y" else Z_SIZE for axis in axes]
                for phase in range(2):
                    length = lengths[phase]
                    offsets = [0]
                    if phase == 1:
                        reach = lengths[0] // 2
                        offsets = list(range(1 - reach, reach + 1)) if eager else [None]
                    for offset in offsets:
                        for step in range(1, length // 2 + 1):
                            for side in range(2):
                                if step > 1:
                                    needs = [(plane, half, phase, offset, step - 1, side)]
                                elif phase == 0:
                                    needs = []
                                else:
                                    needs = [
                                        (plane, half, 0, 0, hop, way)
                                        for hop in range(1, reach + 1)
                                        for way in range(2)
                                        if offset is None
                                        or hop == abs(offset) and (hop == reach or (way == 1) == (offset > 0))
                                    ]
                                size = sizes[half] * (0.5 if step == length // 2 else 1.0)
                                if offset is None:
                                    size *= lengths[0]
                                key = (plane, half, phase, offset, step, side)
                                jobs[key] = (needs, axes[phase], step == length // 2, size)
        return jobs

    def start(self, key, axis, last):
        plane, half, phase, offset, step, side = key
        own, everyone, half_index, side_index, _, _ = self.planes[plane]
        index = half_index(half)
        if last:
            index = side_index(side, index)
        other = axis if phase == 1 else ("y" if axis == "z" else "z")
        back = (step - 1) * (1 if side == 0 else -1)
        if phase == 1:
            at = self.at(axis, back, offset)
        else:
            at = self.at(other, 0, -back)
        place = everyone.at[at + index]
        source = own.at[index] if phase == 0 and step == 1 and own is not None else place
        self.send(key, source, place, {"dp": self.sides[axis][side]})

    def run(self, arrived=None, work=(), work_time=0.0):
        jobs = self.jobs()
        waiting = sorted(jobs, key=lambda key: (key[2], key[4], key[0], key[1]))
        free, flying, here, work = {}, {}, set(), list(work)
        now = 0.0
        while waiting or flying:
            for key in list(waiting):
                needs, axis, last, size = jobs[key]
                if all(need in here for need in needs):
                    self.start(key, axis, last)
                    waiting.remove(key)
                    begin = max(now, free.get((axis, key[5]), 0.0))
                    free[(axis, key[5])] = begin + size / self.RATE
                    flying[key] = begin + size / self.RATE + self.LATENCY
            key = min(flying, key=lambda key: (flying[key], jobs[key][3]))
            while work and flying[key] > now + 0.5 * work_time:
                work.pop(0)()
                now += work_time
            now = max(now, flying.pop(key))
            self.arrive(*key)
            here.add(key)
            if arrived is not None:
                arrived(key, here, jobs)
        for item in work:
            item()

    def finish(self):
        for group in self.copies.values():
            for copy in group:
                copy.wait_send()


def spread_kernel(
    block_ref, x_ref, centroids_ref, out_ref, lowest_ref, send_sem, recv_sem, local_sem, doubled, lowest
):
    width = block_ref.shape[1]
    halves = (pl.ds(0, 32), pl.ds(32, 64))
    plane = (
        block_ref,
        out_ref,
        lambda half: (halves[half], pl.ds(0, width)),
        lambda side, index: (index[0], pl.ds(side * width // 2, width // 2)),
        (32 * width * 2, 64 * width * 2),
        True,
    )
    rings = Rings([plane], send_sem, recv_sem)
    rings.greet()
    pl.semaphore_wait(pltpu.get_barrier_semaphore(), 4)
    own = pltpu.make_async_copy(block_ref, out_ref.at[rings.z, rings.y], local_sem)
    own.start()
    own.wait()
    doubled[...] = x_ref[...] * jnp.bfloat16(-2.0)
    lowest[...] = jnp.full_like(lowest, jnp.inf)
    parts = centroids_ref.shape[0] // 256
    share = parts // 8

    def costs(first):
        def piece_costs(part, carry):
            piece = centroids_ref[pl.ds(pl.multiple_of(part * 256, 256), 256), :]
            wide = piece.astype(jnp.float32)
            norms = jnp.sum(wide * wide, axis=1, keepdims=True)
            values = nt_dot(piece, doubled[...]) + norms
            values = jnp.min(values.reshape(32, 8, values.shape[1]), axis=0)
            lowest[...] = jnp.minimum(lowest[...], values)
            return carry

        lax.fori_loop(first, first + share, piece_costs, 0)

    rings.run(None, [functools.partial(costs, i * share) for i in range(8)], 2.2)
    lowest_ref[...] = jnp.min(lowest[...], axis=0, keepdims=True)
    rings.finish()


def spread(block, embeddings, centroids):
    rows, features = embeddings.shape
    out, lowest = pl.pallas_call(
        spread_kernel,
        in_specs=[
            pl.BlockSpec(memory_space=pl.ANY),
            pl.BlockSpec(memory_space=pltpu.VMEM),
            pl.BlockSpec(memory_space=pltpu.VMEM),
        ],
        out_specs=(pl.BlockSpec(memory_space=pl.ANY), pl.BlockSpec(memory_space=pltpu.VMEM)),
        out_shape=(
            jax.ShapeDtypeStruct((Z_SIZE, Y_SIZE) + block.shape, block.dtype),
            jax.ShapeDtypeStruct((1, rows), jnp.float32),
        ),
        scratch_shapes=[
            pltpu.SemaphoreType.DMA((80,)),
            pltpu.SemaphoreType.DMA((80,)),
            pltpu.SemaphoreType.DMA,
            pltpu.VMEM((rows, features), jnp.bfloat16),
            pltpu.VMEM((8, rows), jnp.float32),
        ],
        compiler_params=pltpu.CompilerParams(
            collective_id=0, has_side_effects=True, vmem_limit_bytes=VMEM_BYTES
        ),
        cost_estimate=pl.CostEstimate(
            flops=2 * rows * features * centroids.shape[0], bytes_accessed=2**24, transcendentals=0
        ),
    )(block, embeddings, centroids)
    return out, lowest[0]


def share_kernel(means_ref, tags_ref, all_means, all_tags, send_sem, recv_sem, local_sem):
    member = lax.axis_index("group")
    x, core = member // 2, member % 2
    means, tags = all_means.at[core], all_tags.at[core]

    def plane(everyone, rows, row_bytes, eager):
        return (
            None,
            everyone,
            lambda half: (slice(None), pl.ds(half * rows, rows)),
            lambda side, index: (pl.ds(side * 2, 2), index[1]),
            (4 * rows * row_bytes, 4 * rows * row_bytes),
            eager,
        )

    planes = [plane(means, 16, 1536, True), plane(tags, 8, 512, False)]
    rings = Rings(planes, send_sem, recv_sem)
    sibling = {"group": x * 2 + 1 - core}
    others = [{"group": lax.rem(x + step, 4) * 2 + core} for step in (1, 2, 3)]
    barrier = pltpu.get_barrier_semaphore()
    rings.greet()
    for other in others + [sibling]:
        pl.semaphore_signal(barrier, inc=1, device_id=other, device_id_type=MESH)
    pl.semaphore_wait(barrier, 8)
    z, y = rings.z, rings.y
    blocks = [(means_ref, means.at[z, y, x]), (tags_ref, tags.at[z, y, x])]
    local = [pltpu.make_async_copy(*block, local_sem.at[i]) for i, block in enumerate(blocks)]
    for copy in local:
        copy.start()
    for other in others:
        for source, place in blocks:
            rings.send(("x",), source, place, other)
    for copy in local:
        copy.wait()
    rings.arrive("x")

    sent = set()

    def to_sibling(key, here, jobs):
        plane, half, phase = key[:3]
        second = "z" if half == 0 else "y"
        reach = (Z_SIZE if second == "z" else Y_SIZE) // 2
        keys = [k for k in jobs if k[:2] == (plane, half)]
        for back in range(1 - reach, reach + 1):
            if back == 0:
                needs = [k for k in keys if k[2] == 0]
            else:
                needs = [
                    k
                    for k in keys
                    if k[2] == 1
                    and k[4] == abs(back)
                    and (abs(back) == reach or (k[5] == 0) == (back > 0))
                ]
            if (plane, half, back) not in sent and all(k in here for k in needs):
                sent.add((plane, half, back))
                _, everyone, half_index, _, _, _ = planes[plane]
                place = everyone.at[rings.at(second, back, None) + half_index(half)]
                rings.send(("core",), place, place, sibling)

    rings.run(to_sibling)
    rings.arrive("core")
    rings.finish()


def share_all(means, tags):
    any_space = pl.BlockSpec(memory_space=pl.ANY)
    return pl.pallas_call(
        share_kernel,
        in_specs=[any_space, any_space],
        out_specs=(any_space, any_space),
        out_shape=(
            jax.ShapeDtypeStruct((2, Z_SIZE, Y_SIZE, 4) + means.shape, means.dtype),
            jax.ShapeDtypeStruct((2, Z_SIZE, Y_SIZE, 4) + tags.shape, tags.dtype),
        ),
        scratch_shapes=[
            pltpu.SemaphoreType.DMA((160,)),
            pltpu.SemaphoreType.DMA((160,)),
            pltpu.SemaphoreType.DMA((2,)),
        ],
        compiler_params=pltpu.CompilerParams(collective_id=1, has_side_effects=True),
        cost_estimate=pl.CostEstimate(flops=0, bytes_accessed=2**24, transcendentals=0),
    )(means, tags)


def scatter_kernel(direct_steps, tags, tag_row_ref, direct_ref, spill_ref, cells_ref, sums_ref, other, combined):
    step = pl.program_id(0)
    tables = (cells_ref, other)

    @pl.when(step == 0)
    def _():
        for table in tables:
            table[...] = jnp.zeros_like(table)

    def add_rows(values):
        batch_of = lambda dim: lax.broadcasted_iota(jnp.int32, (128, 128), dim) // BATCH
        near = batch_of(0) == batch_of(1)
        ones = jnp.ones((32, 128), jnp.bfloat16)
        for block in range(8):
            tag = jnp.broadcast_to(tag_row_ref[0, :, block * 128 : (block + 1) * 128], (128, 128))
            same = jnp.where((tag == tag.T) & near, 1.0, 0.0).astype(jnp.bfloat16)
            combined[block * 128 : (block + 1) * 128, :] = nt_dot(
                same, jnp.concatenate([values(block), ones], axis=0)
            )
        held = None
        for batch in range(1024 // BATCH + 1):
            fresh = []
            for u in range(BATCH):
                if batch < 1024 // BATCH:
                    row = batch * BATCH + u
                    at = tags[0, 0, row]
                    sums = tables[batch % 2][pl.ds(at, 1), :] + combined[row : row + 1, :]
                    fresh.append((at, sums))
                if held is not None:
                    tables[1 - batch % 2][pl.ds(held[u][0], 1), :] = held[u][1]
            held = fresh

    @pl.when(step < direct_steps)
    def _():
        add_rows(lambda block: direct_ref[block // 2, :, block % 2 * 128 : (block % 2 + 1) * 128])

    @pl.when(step >= direct_steps)
    def _():
        add_rows(lambda block: spill_ref[0, :, block * 128 : (block + 1) * 128])

    @pl.when(step == pl.num_programs(0) - 1)
    def _():
        def slot_sums(group, carry):
            for u in range(8):
                at = pl.ds(pl.multiple_of((group * 8 + u) * SUB, SUB), SUB)
                rows = cells_ref[at, :] + other[at, :]
                cells_ref[at, :] = rows
                sums_ref[pl.ds(group * 8 + u, 1), :] = jnp.sum(rows, axis=0, keepdims=True)
            return carry

        lax.fori_loop(0, sums_ref.shape[0] // 8, slot_sums, 0)


def scatter(tags, direct, spilled, slots):
    direct_steps = direct.shape[0] // 4
    spill_steps = spilled.shape[0]
    share = direct.shape[1]
    return pl.pallas_call(
        functools.partial(scatter_kernel, direct_steps),
        grid=(direct_steps + spill_steps,),
        in_specs=[
            pl.BlockSpec((1, 1, 1024), lambda i: (i, 0, 0), memory_space=pltpu.SMEM),
            pl.BlockSpec((1, 1, 1024), lambda i: (i, 0, 0)),
            pl.BlockSpec((4, share, 256), lambda i: (jnp.minimum(i, direct_steps - 1), 0, 0)),
            pl.BlockSpec((1, share, 1024), lambda i: (jnp.maximum(i - direct_steps, 0), 0, 0)),
        ],
        out_specs=(
            pl.BlockSpec((slots * SUB + 8, 128), lambda i: (0, 0)),
            pl.BlockSpec((slots, 128), lambda i: (0, 0)),
        ),
        out_shape=(
            jax.ShapeDtypeStruct((slots * SUB + 8, 128), jnp.float32),
            jax.ShapeDtypeStruct((slots, 128), jnp.float32),
        ),
        scratch_shapes=[
            pltpu.VMEM((slots * SUB + 8, 128), jnp.float32),
            pltpu.VMEM((1024, 128), jnp.float32),
        ],
        compiler_params=pltpu.CompilerParams(vmem_limit_bytes=VMEM_BYTES),
    )(tags, tags, direct, spilled)


def update_kernel(cells_ref, old_ref, out_ref, turned, counts):
    first = lax.broadcasted_iota(jnp.int32, (48, 128), 1) < SUB
    first_row = first[0:1]
    for pair in range(8):
        block = cells_ref[pair * 128 : (pair + 1) * 128, :].T
        rolled = pltpu.roll(block, SUB, 1)
        even = jnp.where(first, block[0:48], rolled[48:96])
        odd = jnp.where(first, rolled[0:48], block[48:96])
        slot = 2 * pair
        turned[slot // 8, pl.ds(slot % 8, 48, stride=8), :] = even
        turned[slot // 8, pl.ds(slot % 8 + 1, 48, stride=8), :] = odd
        counts[slot : slot + 1, :] = jnp.where(first_row, block[96:97], rolled[96:97])
        counts[slot + 1 : slot + 2, :] = jnp.where(first_row, rolled[96:97], block[96:97])
    scale = 1.0 / (counts[...] + 1.0)
    for tile in range(48):
        sums = jnp.concatenate(
            [turned[0, tile * 8 : (tile + 1) * 8, :], turned[1, tile * 8 : (tile + 1) * 8, :]], axis=0
        )
        old = old_ref[:, tile * 128 : (tile + 1) * 128].astype(jnp.float32)
        out_ref[:, tile * 128 : (tile + 1) * 128] = ((sums + old) * scale).astype(jnp.bfloat16)


def update(cells, fine_means):
    slots, width = fine_means.shape
    return pl.pallas_call(
        update_kernel,
        grid=(slots // 16,),
        in_specs=[
            pl.BlockSpec((16 * SUB, 128), lambda i: (i, 0)),
            pl.BlockSpec((16, width), lambda i: (i, 0)),
        ],
        out_specs=pl.BlockSpec((16, width), lambda i: (i, 0)),
        out_shape=jax.ShapeDtypeStruct((slots, width), jnp.bfloat16),
        scratch_shapes=[pltpu.VMEM((2, 48 * 8, 128), jnp.float32), pltpu.VMEM((16, 128), jnp.float32)],
        compiler_params=pltpu.CompilerParams(vmem_limit_bytes=VMEM_BYTES),
        cost_estimate=pl.CostEstimate(flops=2**24, bytes_accessed=2**24, transcendentals=0),
    )(cells, fine_means)


def on_device(embeddings, coarse_label, fine_label, slot_table, coarse_means, fine_means):
    row_count, feature_count = embeddings.shape
    owner_count = lax.axis_size("dp")
    member_count = lax.axis_size("group")
    slots = fine_means.shape[0]
    share = feature_count // member_count
    table_cells = slots * SUB
    me = lax.axis_index("dp")

    slot_index = jnp.take(slot_table, coarse_label)
    owner_index = slot_index // slots
    matches = owner_index[:, None] == jnp.arange(owner_count, dtype=jnp.int32)[None, :]
    row_ids = jnp.arange(row_count, dtype=jnp.int32)
    before = (row_ids[:, None] > row_ids[None, :]).astype(jnp.bfloat16)
    earlier = jnp.dot(before, matches.astype(jnp.bfloat16), preferred_element_type=jnp.float32)
    excess = jnp.maximum(jnp.sum(matches.astype(jnp.int32), axis=0) - DIRECT, 0)
    offsets = jnp.cumsum(excess) - excess
    excess_total = jnp.sum(excess)
    rank = jnp.sum(jnp.where(matches, earlier, 0.0), axis=1).astype(jnp.int32)
    offset = jnp.sum(jnp.where(matches, offsets[None, :], 0), axis=1)
    direct_width = owner_count * DIRECT
    position = jnp.where(
        rank < DIRECT, owner_index * DIRECT + rank, direct_width + offset + rank - DIRECT
    )
    cell = slot_index * SUB + fine_label
    width = direct_width + SPILL

    def tags_at(position_ids):
        hits = position[None, :] == position_ids[:, None]
        return jnp.sum(jnp.where(hits, cell[None, :] + 1, 0), axis=1)

    tags = jnp.concatenate(
        [
            tags_at(jnp.arange(width, dtype=jnp.int32)).reshape(-1, 128),
            jnp.broadcast_to(excess_total, (16 - width // 128, 128)),
        ],
        axis=0,
    )
    packed = pack(embeddings, position, width).reshape(member_count, share, width)
    packed, tags = lax.optimization_barrier((packed, tags))
    arrived = lax.all_to_all(packed, "group", split_axis=0, concat_axis=0, tiled=True)
    centroids, all_tags = share_all(coarse_means, tags)
    arrived, centroids, all_tags = lax.optimization_barrier((arrived, centroids, all_tags))
    direct, spill = regroup(arrived, owner_count)
    direct = lax.all_to_all(direct, "dp", split_axis=0, concat_axis=0, tiled=True)
    own_norms = jnp.sum(jnp.square(embeddings.astype(jnp.float32)), axis=1)
    spilled, lowest = spread(spill, embeddings, centroids.reshape(-1, feature_count))
    spilled = spilled.reshape(owner_count, share, member_count * SPILL)
    nearest_cost = (own_norms + lowest) / feature_count

    def local_cells(global_tags):
        local = global_tags - 1 - me * table_cells
        return jnp.where((local >= 0) & (local < table_cells), local, table_cells)

    all_tags = all_tags.reshape(2, owner_count, 4, 16, 128)
    per_line = 128 // DIRECT
    direct_tags = lax.dynamic_slice_in_dim(all_tags, me // per_line, 1, axis=3)
    direct_tags = lax.dynamic_slice_in_dim(direct_tags, me % per_line * DIRECT, DIRECT, axis=4)
    spill_tags = all_tags[:, :, :, direct_width // 128]
    step_tags = jnp.concatenate(
        [
            direct_tags.reshape(2, owner_count, 4, DIRECT).transpose(1, 2, 0, 3).reshape(-1, 1, 1024),
            spill_tags.transpose(1, 2, 0, 3).reshape(-1, 1, 1024),
        ],
        axis=0,
    )
    cells, sums = scatter(local_cells(step_tags), direct, spilled, slots)
    rounds = (jnp.max(all_tags[:, :, :, width // 128, 0]) + SPILL - 1) // SPILL

    def more(state):
        return state[0] < rounds

    def another_round(state):
        number, cells, sums = state
        ids = direct_width + number * SPILL + jnp.arange(SPILL, dtype=jnp.int32)
        hits = (position[None, :] == ids[:, None]).astype(jnp.bfloat16)
        rows = jnp.dot(hits, embeddings, preferred_element_type=jnp.float32).astype(jnp.bfloat16)
        rows = rows.reshape(SPILL, member_count, share // 2, 2).transpose(1, 0, 3, 2)
        rows = rows.reshape(member_count, SPILL, share)
        rows = lax.all_to_all(rows, "group", split_axis=0, concat_axis=0, tiled=True)
        rows = lax.all_gather(rows, "dp", axis=0, tiled=True).reshape(-1, share)
        round_cells = lax.all_gather(tags_at(ids), ("dp", "group"), axis=0, tiled=True)
        round_cells = local_cells(round_cells)
        ones = jnp.ones((rows.shape[0], 128 - share), jnp.float32)
        rows = jnp.concatenate([rows.astype(jnp.float32), ones], axis=1)
        cells = cells.at[round_cells].add(rows)
        sums = sums + jax.ops.segment_sum(rows, round_cells // SUB, num_segments=slots + 1)[:slots]
        return number + 1, cells, sums

    _, cells, sums = lax.while_loop(more, another_round, (jnp.int32(1), cells, sums))

    own = lax.all_to_all(
        sums.reshape(member_count, -1, 128), "group", split_axis=0, concat_axis=0, tiled=True
    )
    fine_update = update(cells, fine_means)
    own_count = own[0, :, share]
    own_sums = own[:, :, :share].reshape(member_count, -1, 2, share // 2)
    own_sums = own_sums.transpose(1, 0, 3, 2).reshape(-1, feature_count)
    coarse_update = (
        (own_sums + coarse_means.astype(jnp.float32)) / (own_count[:, None] + 1.0)
    ).astype(jnp.bfloat16)

    return (coarse_update, fine_update, nearest_cost)


def solution(mesh):
    placed = (
        P(("dp", "group"), None),
        P(("dp", "group")),
        P(("dp", "group")),
        P(),
        P(("dp", "group"), None),
        P("dp", "group"),
    )
    return jax.shard_map(
        on_device,
        mesh=mesh,
        in_specs=placed,
        out_specs=(P(("dp", "group"), None), P("dp", "group"), P(("dp", "group"))),
        check_vma=False,
    )
```

```python
import functools

import jax
import jax.numpy as jnp
from jax import lax
from jax.experimental import pallas as pl
from jax.experimental.pallas import tpu as pltpu
from jax.sharding import PartitionSpec as P

SUB = 64
DIRECT = 32
SPILL = 128
SPILL_FRONT = 96
BATCH = 8
Z_SIZE, Y_SIZE = 8, 4
VMEM_BYTES = 56 * 2**20
MESH = pl.DeviceIdType.MESH


def nt_dot(left, right):
    return lax.dot_general(left, right, (((1,), (1,)), ((), ())), preferred_element_type=jnp.float32)


def pack_kernel(x_ref, position_ref, out_ref, turned):
    features = x_ref.shape[1]
    share = 96
    k = lax.broadcasted_iota(jnp.int32, (features, features), 0)
    within = k % share
    feature = k - within + jnp.where(within < share // 2, 2 * within, 2 * within - share + 1)
    select = feature == lax.broadcasted_iota(jnp.int32, (features, features), 1)
    select = jnp.where(select, 1.0, 0.0).astype(jnp.bfloat16)
    turned[...] = nt_dot(select, x_ref[...]).astype(jnp.bfloat16)
    positions = position_ref[...]
    for tile in range(out_ref.shape[1] // 128):
        ids = tile * 128 + lax.broadcasted_iota(jnp.int32, (128, positions.shape[1]), 0)
        hits = jnp.where(positions == ids, 1.0, 0.0).astype(jnp.bfloat16)
        out_ref[:, tile * 128 : (tile + 1) * 128] = nt_dot(turned[...], hits).astype(jnp.bfloat16)


def pack(embeddings, position, width):
    rows, features = embeddings.shape
    return pl.pallas_call(
        pack_kernel,
        out_shape=jax.ShapeDtypeStruct((features, width), jnp.bfloat16),
        scratch_shapes=[pltpu.VMEM((features, rows), jnp.bfloat16)],
        compiler_params=pltpu.CompilerParams(vmem_limit_bytes=VMEM_BYTES),
    )(embeddings, position.reshape(1, rows))


def regroup_kernel(in_ref, direct_ref, spill_ref):
    members = in_ref.shape[0]
    quads = direct_ref.shape[0] // 4
    to = lax.broadcasted_iota(jnp.int32, (512, 512), 0)
    source = (to // DIRECT) % 4 * 128 + to // 128 * DIRECT + to % DIRECT
    move = source == lax.broadcasted_iota(jnp.int32, (512, 512), 1)
    move = jnp.where(move, 1.0, 0.0).astype(jnp.bfloat16)
    for half in range(members // 4):
        for quad in range(quads):
            block = jnp.concatenate(
                [in_ref[half * 4 + m, :, quad * 128 : (quad + 1) * 128] for m in range(4)], axis=1
            )
            moved = nt_dot(block, move).astype(jnp.bfloat16)
            for i in range(4):
                direct_ref[quad * 4 + i, :, half * 128 : (half + 1) * 128] = moved[
                    :, i * 128 : (i + 1) * 128
                ]
    for m in range(members):
        spill_ref[:, m * SPILL : (m + 1) * SPILL] = in_ref[m, :, quads * 128 :]


def regroup(arrived, owners):
    members, share, _ = arrived.shape
    return pl.pallas_call(
        regroup_kernel,
        out_shape=(
            jax.ShapeDtypeStruct((owners, share, members * DIRECT), jnp.bfloat16),
            jax.ShapeDtypeStruct((share, members * SPILL), jnp.bfloat16),
        ),
        compiler_params=pltpu.CompilerParams(vmem_limit_bytes=VMEM_BYTES),
    )(arrived)


class Rings:
    RATE, LATENCY = 50e3, 2.0

    def __init__(self, planes, send_sem, recv_sem):
        me = lax.axis_index("dp")
        self.z, self.y = me // Y_SIZE, me % Y_SIZE
        self.planes, self.send_sem, self.recv_sem = planes, send_sem, recv_sem
        self.copies, self.count = {}, 0
        z, y = self.z, self.y
        self.sides = {
            "y": (self.owner(z, y + 1), self.owner(z, y - 1)),
            "z": (self.owner(z + 1, y), self.owner(z - 1, y)),
        }

    @staticmethod
    def owner(z_at, y_at):
        return lax.rem(z_at + Z_SIZE, Z_SIZE) * Y_SIZE + lax.rem(y_at + Y_SIZE, Y_SIZE)

    def greet(self):
        barrier = pltpu.get_barrier_semaphore()
        for axis in "yz":
            for side in self.sides[axis]:
                pl.semaphore_signal(barrier, inc=1, device_id={"dp": side}, device_id_type=MESH)

    def at(self, second, back, offset):
        z_shift, y_shift = (-back, offset) if second == "z" else (offset, -back)
        at_z = slice(None) if z_shift is None else lax.rem(self.z + z_shift + Z_SIZE, Z_SIZE)
        at_y = slice(None) if y_shift is None else lax.rem(self.y + y_shift + Y_SIZE, Y_SIZE)
        return (at_z, at_y)

    def send(self, key, source, place, device):
        copy = pltpu.make_async_remote_copy(
            src_ref=source,
            dst_ref=place,
            send_sem=self.send_sem.at[self.count],
            recv_sem=self.recv_sem.at[self.count],
            device_id=device,
            device_id_type=MESH,
        )
        self.count += 1
        copy.start()
        self.copies.setdefault(key, []).append(copy)

    def arrive(self, *key):
        for copy in self.copies[key]:
            copy.wait_recv()

    def jobs(self):
        jobs = {}
        for plane, (_, _, _, _, sizes, eager) in enumerate(self.planes):
            for half in range(2):
                axes = "yz" if half == 0 else "zy"
                lengths = [Y_SIZE if axis == "y" else Z_SIZE for axis in axes]
                for phase in range(2):
                    length = lengths[phase]
                    offsets = [0]
                    if phase == 1:
                        reach = lengths[0] // 2
                        offsets = list(range(1 - reach, reach + 1)) if eager else [None]
                    for offset in offsets:
                        for step in range(1, length // 2 + 1):
                            for side in range(2):
                                if step > 1:
                                    needs = [(plane, half, phase, offset, step - 1, side)]
                                elif phase == 0:
                                    needs = []
                                else:
                                    needs = [
                                        (plane, half, 0, 0, hop, way)
                                        for hop in range(1, reach + 1)
                                        for way in range(2)
                                        if offset is None
                                        or hop == abs(offset) and (hop == reach or (way == 1) == (offset > 0))
                                    ]
                                size = sizes[half] * (0.5 if step == length // 2 else 1.0)
                                if offset is None:
                                    size *= lengths[0]
                                key = (plane, half, phase, offset, step, side)
                                jobs[key] = (needs, axes[phase], step == length // 2, size)
        return jobs

    def start(self, key, axis, last):
        plane, half, phase, offset, step, side = key
        own, everyone, half_index, side_index, _, _ = self.planes[plane]
        index = half_index(half)
        if last:
            index = side_index(side, index)
        other = axis if phase == 1 else ("y" if axis == "z" else "z")
        back = (step - 1) * (1 if side == 0 else -1)
        if phase == 1:
            at = self.at(axis, back, offset)
        else:
            at = self.at(other, 0, -back)
        place = everyone.at[at + index]
        source = own.at[index] if phase == 0 and step == 1 and own is not None else place
        self.send(key, source, place, {"dp": self.sides[axis][side]})

    def run(self, arrived=None, work=(), work_time=0.0):
        jobs = self.jobs()
        waiting = sorted(jobs, key=lambda key: (key[2], key[4], key[0], key[1]))
        free, flying, here, work = {}, {}, set(), list(work)
        now = 0.0
        while waiting or flying:
            for key in list(waiting):
                needs, axis, last, size = jobs[key]
                if all(need in here for need in needs):
                    self.start(key, axis, last)
                    waiting.remove(key)
                    begin = max(now, free.get((axis, key[5]), 0.0))
                    free[(axis, key[5])] = begin + size / self.RATE
                    flying[key] = begin + size / self.RATE + self.LATENCY
            key = min(flying, key=lambda key: (flying[key], jobs[key][3]))
            while work and flying[key] > now + 0.5 * work_time:
                work.pop(0)()
                now += work_time
            now = max(now, flying.pop(key))
            self.arrive(*key)
            here.add(key)
            if arrived is not None:
                arrived(key, here, jobs)
        for item in work:
            item()

    def finish(self):
        for group in self.copies.values():
            for copy in group:
                copy.wait_send()


def spread_kernel(
    block_ref, x_ref, centroids_ref, out_ref, lowest_ref, send_sem, recv_sem, local_sem, doubled, lowest
):
    width = block_ref.shape[1]
    halves = (pl.ds(0, 32), pl.ds(32, 64))
    plane = (
        block_ref,
        out_ref,
        lambda half: (halves[half], pl.ds(0, width)),
        lambda side, index: (index[0], pl.ds(side * width // 2, width // 2)),
        (32 * width * 2, 64 * width * 2),
        True,
    )
    rings = Rings([plane], send_sem, recv_sem)
    rings.greet()
    pl.semaphore_wait(pltpu.get_barrier_semaphore(), 4)
    own = pltpu.make_async_copy(block_ref, out_ref.at[rings.z, rings.y], local_sem)
    own.start()
    own.wait()
    doubled[...] = x_ref[...] * jnp.bfloat16(-2.0)
    lowest[...] = jnp.full_like(lowest, jnp.inf)
    parts = centroids_ref.shape[0] // 256
    share = parts // 8

    def costs(first):
        def piece_costs(part, carry):
            piece = centroids_ref[pl.ds(pl.multiple_of(part * 256, 256), 256), :]
            wide = piece.astype(jnp.float32)
            norms = jnp.sum(wide * wide, axis=1, keepdims=True)
            values = nt_dot(piece, doubled[...]) + norms
            values = jnp.min(values.reshape(32, 8, values.shape[1]), axis=0)
            lowest[...] = jnp.minimum(lowest[...], values)
            return carry

        lax.fori_loop(first, first + share, piece_costs, 0)

    rings.run(None, [functools.partial(costs, i * share) for i in range(8)], 2.2)
    lowest_ref[...] = jnp.min(lowest[...], axis=0, keepdims=True)
    rings.finish()


def spread(block, embeddings, centroids):
    rows, features = embeddings.shape
    out, lowest = pl.pallas_call(
        spread_kernel,
        in_specs=[
            pl.BlockSpec(memory_space=pl.ANY),
            pl.BlockSpec(memory_space=pltpu.VMEM),
            pl.BlockSpec(memory_space=pltpu.VMEM),
        ],
        out_specs=(pl.BlockSpec(memory_space=pl.ANY), pl.BlockSpec(memory_space=pltpu.VMEM)),
        out_shape=(
            jax.ShapeDtypeStruct((Z_SIZE, Y_SIZE) + block.shape, block.dtype),
            jax.ShapeDtypeStruct((1, rows), jnp.float32),
        ),
        scratch_shapes=[
            pltpu.SemaphoreType.DMA((80,)),
            pltpu.SemaphoreType.DMA((80,)),
            pltpu.SemaphoreType.DMA,
            pltpu.VMEM((rows, features), jnp.bfloat16),
            pltpu.VMEM((8, rows), jnp.float32),
        ],
        compiler_params=pltpu.CompilerParams(
            collective_id=0, has_side_effects=True, vmem_limit_bytes=VMEM_BYTES
        ),
        cost_estimate=pl.CostEstimate(
            flops=2 * rows * features * centroids.shape[0], bytes_accessed=2**24, transcendentals=0
        ),
    )(block, embeddings, centroids)
    return out, lowest[0]


def share_kernel(means_ref, tags_ref, all_means, all_tags, send_sem, recv_sem, local_sem):
    member = lax.axis_index("group")
    x, core = member // 2, member % 2
    means, tags = all_means.at[core], all_tags.at[core]

    def plane(everyone, rows, row_bytes, eager):
        return (
            None,
            everyone,
            lambda half: (slice(None), pl.ds(half * rows, rows)),
            lambda side, index: (pl.ds(side * 2, 2), index[1]),
            (4 * rows * row_bytes, 4 * rows * row_bytes),
            eager,
        )

    planes = [plane(means, 16, 1536, True), plane(tags, 8, 512, False)]
    rings = Rings(planes, send_sem, recv_sem)
    sibling = {"group": x * 2 + 1 - core}
    others = [{"group": lax.rem(x + step, 4) * 2 + core} for step in (1, 2, 3)]
    barrier = pltpu.get_barrier_semaphore()
    rings.greet()
    for other in others + [sibling]:
        pl.semaphore_signal(barrier, inc=1, device_id=other, device_id_type=MESH)
    pl.semaphore_wait(barrier, 8)
    z, y = rings.z, rings.y
    blocks = [(means_ref, means.at[z, y, x]), (tags_ref, tags.at[z, y, x])]
    local = [pltpu.make_async_copy(*block, local_sem.at[i]) for i, block in enumerate(blocks)]
    for copy in local:
        copy.start()
    for other in others:
        for source, place in blocks:
            rings.send(("x",), source, place, other)
    for copy in local:
        copy.wait()
    rings.arrive("x")

    sent = set()

    def to_sibling(key, here, jobs):
        plane, half, phase = key[:3]
        second = "z" if half == 0 else "y"
        reach = (Z_SIZE if second == "z" else Y_SIZE) // 2
        keys = [k for k in jobs if k[:2] == (plane, half)]
        for back in range(1 - reach, reach + 1):
            if back == 0:
                needs = [k for k in keys if k[2] == 0]
            else:
                needs = [
                    k
                    for k in keys
                    if k[2] == 1
                    and k[4] == abs(back)
                    and (abs(back) == reach or (k[5] == 0) == (back > 0))
                ]
            if (plane, half, back) not in sent and all(k in here for k in needs):
                sent.add((plane, half, back))
                _, everyone, half_index, _, _, _ = planes[plane]
                place = everyone.at[rings.at(second, back, None) + half_index(half)]
                rings.send(("core",), place, place, sibling)

    rings.run(to_sibling)
    rings.arrive("core")
    rings.finish()


def share_all(means, tags):
    any_space = pl.BlockSpec(memory_space=pl.ANY)
    return pl.pallas_call(
        share_kernel,
        in_specs=[any_space, any_space],
        out_specs=(any_space, any_space),
        out_shape=(
            jax.ShapeDtypeStruct((2, Z_SIZE, Y_SIZE, 4) + means.shape, means.dtype),
            jax.ShapeDtypeStruct((2, Z_SIZE, Y_SIZE, 4) + tags.shape, tags.dtype),
        ),
        scratch_shapes=[
            pltpu.SemaphoreType.DMA((160,)),
            pltpu.SemaphoreType.DMA((160,)),
            pltpu.SemaphoreType.DMA((2,)),
        ],
        compiler_params=pltpu.CompilerParams(collective_id=1, has_side_effects=True),
        cost_estimate=pl.CostEstimate(flops=0, bytes_accessed=2**24, transcendentals=0),
    )(means, tags)


def scatter_kernel(direct_steps, tags, flags, direct_ref, spill_ref, cells_ref, sums_ref, other, turned):
    step = pl.program_id(0)
    tables = (cells_ref, other)

    @pl.when(step == 0)
    def _():
        for table in tables:
            table[...] = jnp.zeros_like(table)

    def add_batches(first, end):
        held = None
        for batch in range(first, end + 1):
            fresh = []
            for u in range(BATCH):
                if batch < end:
                    row = u * 128 + batch
                    at = tags[0, 0, row]
                    sums = tables[batch % 2][pl.ds(at, 1), :] + turned[row : row + 1, :]
                    fresh.append((at, sums))
                if held is not None:
                    tables[1 - batch % 2][pl.ds(held[u][0], 1), :] = held[u][1]
            held = fresh

    def add_rows(values, always):
        ones = jnp.ones((32, 128), jnp.float32)
        for block in range(BATCH):
            turned[block * 128 : (block + 1) * 128, :] = jnp.concatenate(
                [values(block).astype(jnp.float32), ones], axis=0
            ).T
        add_batches(0, always)
        if always < 128:

            @pl.when(flags[0, 0, 2] > 0)
            def _():
                add_batches(always, 128)

        def add_repeated(batch, carry):
            for u in range(1, BATCH):
                at = tags[0, 1, u * 128 + batch]
                cells_ref[pl.ds(at, 1), :] += turned[pl.ds(u * 128 + batch, 1), :]
            return carry

        lax.fori_loop(flags[0, 0, 0], flags[0, 0, 1], add_repeated, 0)

    @pl.when(step < direct_steps)
    def _():
        add_rows(lambda block: direct_ref[block // 2, :, block % 2 * 128 : (block % 2 + 1) * 128], 128)

    @pl.when(step >= direct_steps)
    def _():
        add_rows(lambda block: spill_ref[0, :, block * 128 : (block + 1) * 128], SPILL_FRONT)

    @pl.when(step == pl.num_programs(0) - 1)
    def _():
        def slot_sums(group, carry):
            for u in range(8):
                at = pl.ds(pl.multiple_of((group * 8 + u) * SUB, SUB), SUB)
                rows = cells_ref[at, :] + other[at, :]
                cells_ref[at, :] = rows
                sums_ref[pl.ds(group * 8 + u, 1), :] = jnp.sum(rows, axis=0, keepdims=True)
            return carry

        lax.fori_loop(0, sums_ref.shape[0] // 8, slot_sums, 0)


def scatter(tags, direct, spilled, slots):
    direct_steps = direct.shape[0] // 4
    spill_steps = spilled.shape[0]
    share = direct.shape[1]
    steps = direct_steps + spill_steps
    nowhere = slots * SUB
    earlier = jnp.arange(BATCH)[:, None] > jnp.arange(BATCH)[None, :]
    repeated = (tags[:, :, None] == tags[:, None, :]) & earlier[None, :, :, None]
    repeated = jnp.any(repeated, axis=2) & (tags < nowhere)
    planes = jnp.stack(
        [jnp.where(repeated, nowhere, tags), jnp.where(repeated, tags, nowhere)], axis=1
    ).reshape(steps, 2, 1024)
    at_batch = jnp.arange(128, dtype=jnp.int32)
    first = jnp.min(jnp.where(repeated, at_batch, 128), axis=(1, 2))
    last = jnp.max(jnp.where(repeated, at_batch + 1, 0), axis=(1, 2))
    tail = jnp.any(tags[:, :, SPILL_FRONT:] < nowhere, axis=(1, 2)).astype(jnp.int32)
    flags = jnp.stack([first, last, tail], axis=1)
    flags = jnp.pad(flags, ((0, 0), (0, 125))).reshape(steps, 1, 128)
    return pl.pallas_call(
        functools.partial(scatter_kernel, direct_steps),
        grid=(steps,),
        in_specs=[
            pl.BlockSpec((1, 2, 1024), lambda i: (i, 0, 0), memory_space=pltpu.SMEM),
            pl.BlockSpec((1, 1, 128), lambda i: (i, 0, 0), memory_space=pltpu.SMEM),
            pl.BlockSpec((4, share, 256), lambda i: (jnp.minimum(i, direct_steps - 1), 0, 0)),
            pl.BlockSpec((1, share, 1024), lambda i: (jnp.maximum(i - direct_steps, 0), 0, 0)),
        ],
        out_specs=(
            pl.BlockSpec((slots * SUB + 8, 128), lambda i: (0, 0)),
            pl.BlockSpec((slots, 128), lambda i: (0, 0)),
        ),
        out_shape=(
            jax.ShapeDtypeStruct((slots * SUB + 8, 128), jnp.float32),
            jax.ShapeDtypeStruct((slots, 128), jnp.float32),
        ),
        scratch_shapes=[
            pltpu.VMEM((slots * SUB + 8, 128), jnp.float32),
            pltpu.VMEM((1024, 128), jnp.float32),
        ],
        compiler_params=pltpu.CompilerParams(vmem_limit_bytes=VMEM_BYTES),
    )(planes, flags, direct, spilled)


def update_kernel(cells_ref, old_ref, out_ref, turned, counts):
    first = lax.broadcasted_iota(jnp.int32, (48, 128), 1) < SUB
    first_row = first[0:1]
    for pair in range(8):
        block = cells_ref[pair * 128 : (pair + 1) * 128, :].T
        rolled = pltpu.roll(block, SUB, 1)
        even = jnp.where(first, block[0:48], rolled[48:96])
        odd = jnp.where(first, rolled[0:48], block[48:96])
        slot = 2 * pair
        turned[slot // 8, pl.ds(slot % 8, 48, stride=8), :] = even
        turned[slot // 8, pl.ds(slot % 8 + 1, 48, stride=8), :] = odd
        counts[slot : slot + 1, :] = jnp.where(first_row, block[96:97], rolled[96:97])
        counts[slot + 1 : slot + 2, :] = jnp.where(first_row, rolled[96:97], block[96:97])
    scale = 1.0 / (counts[...] + 1.0)
    for tile in range(48):
        sums = jnp.concatenate(
            [turned[0, tile * 8 : (tile + 1) * 8, :], turned[1, tile * 8 : (tile + 1) * 8, :]], axis=0
        )
        old = old_ref[:, tile * 128 : (tile + 1) * 128].astype(jnp.float32)
        out_ref[:, tile * 128 : (tile + 1) * 128] = ((sums + old) * scale).astype(jnp.bfloat16)


def update(cells, fine_means):
    slots, width = fine_means.shape
    return pl.pallas_call(
        update_kernel,
        grid=(slots // 16,),
        in_specs=[
            pl.BlockSpec((16 * SUB, 128), lambda i: (i, 0)),
            pl.BlockSpec((16, width), lambda i: (i, 0)),
        ],
        out_specs=pl.BlockSpec((16, width), lambda i: (i, 0)),
        out_shape=jax.ShapeDtypeStruct((slots, width), jnp.bfloat16),
        scratch_shapes=[pltpu.VMEM((2, 48 * 8, 128), jnp.float32), pltpu.VMEM((16, 128), jnp.float32)],
        compiler_params=pltpu.CompilerParams(vmem_limit_bytes=VMEM_BYTES),
        cost_estimate=pl.CostEstimate(flops=2**24, bytes_accessed=2**24, transcendentals=0),
    )(cells, fine_means)


def on_device(embeddings, coarse_label, fine_label, slot_table, coarse_means, fine_means):
    row_count, feature_count = embeddings.shape
    owner_count = lax.axis_size("dp")
    member_count = lax.axis_size("group")
    slots = fine_means.shape[0]
    share = feature_count // member_count
    table_cells = slots * SUB
    me = lax.axis_index("dp")

    slot_index = jnp.take(slot_table, coarse_label)
    owner_index = slot_index // slots
    matches = owner_index[:, None] == jnp.arange(owner_count, dtype=jnp.int32)[None, :]
    row_ids = jnp.arange(row_count, dtype=jnp.int32)
    before = (row_ids[:, None] > row_ids[None, :]).astype(jnp.bfloat16)
    earlier = jnp.dot(before, matches.astype(jnp.bfloat16), preferred_element_type=jnp.float32)
    excess = jnp.maximum(jnp.sum(matches.astype(jnp.int32), axis=0) - DIRECT, 0)
    owner_ids = jnp.arange(owner_count, dtype=jnp.int32)
    ahead = (excess[None, :] > excess[:, None]) | (
        (excess[None, :] == excess[:, None]) & (owner_ids[None, :] < owner_ids[:, None])
    )
    offsets = jnp.sum(jnp.where(ahead, excess[None, :], 0), axis=1)
    excess_total = jnp.sum(excess)
    rank = jnp.sum(jnp.where(matches, earlier, 0.0), axis=1).astype(jnp.int32)
    offset = jnp.sum(jnp.where(matches, offsets[None, :], 0), axis=1)
    direct_width = owner_count * DIRECT
    position = jnp.where(
        rank < DIRECT, owner_index * DIRECT + rank, direct_width + offset + rank - DIRECT
    )
    cell = slot_index * SUB + fine_label
    width = direct_width + SPILL

    def tags_at(position_ids):
        hits = position[None, :] == position_ids[:, None]
        return jnp.sum(jnp.where(hits, cell[None, :] + 1, 0), axis=1)

    tags = jnp.concatenate(
        [
            tags_at(jnp.arange(width, dtype=jnp.int32)).reshape(-1, 128),
            jnp.broadcast_to(excess_total, (16 - width // 128, 128)),
        ],
        axis=0,
    )
    packed = pack(embeddings, position, width).reshape(member_count, share, width)
    packed, tags = lax.optimization_barrier((packed, tags))
    arrived = lax.all_to_all(packed, "group", split_axis=0, concat_axis=0, tiled=True)
    centroids, all_tags = share_all(coarse_means, tags)
    arrived, centroids, all_tags = lax.optimization_barrier((arrived, centroids, all_tags))
    direct, spill = regroup(arrived, owner_count)
    direct = lax.all_to_all(direct, "dp", split_axis=0, concat_axis=0, tiled=True)
    own_norms = jnp.sum(jnp.square(embeddings.astype(jnp.float32)), axis=1)
    spilled, lowest = spread(spill, embeddings, centroids.reshape(-1, feature_count))
    spilled = spilled.reshape(owner_count, share, member_count * SPILL)
    nearest_cost = (own_norms + lowest) / feature_count

    def local_cells(global_tags):
        local = global_tags - 1 - me * table_cells
        return jnp.where((local >= 0) & (local < table_cells), local, table_cells)

    all_tags = all_tags.reshape(2, owner_count, 4, 16, 128)
    per_line = 128 // DIRECT
    direct_tags = lax.dynamic_slice_in_dim(all_tags, me // per_line, 1, axis=3)
    direct_tags = lax.dynamic_slice_in_dim(direct_tags, me % per_line * DIRECT, DIRECT, axis=4)
    spill_tags = all_tags[:, :, :, direct_width // 128]
    step_tags = jnp.concatenate(
        [
            direct_tags.reshape(2, owner_count, 4, DIRECT).transpose(1, 2, 0, 3).reshape(-1, 8, 128),
            spill_tags.transpose(1, 2, 0, 3).reshape(-1, 8, 128),
        ],
        axis=0,
    )
    cells, sums = scatter(local_cells(step_tags), direct, spilled, slots)
    rounds = (jnp.max(all_tags[:, :, :, width // 128, 0]) + SPILL - 1) // SPILL

    def more(state):
        return state[0] < rounds

    def another_round(state):
        number, cells, sums = state
        ids = direct_width + number * SPILL + jnp.arange(SPILL, dtype=jnp.int32)
        hits = (position[None, :] == ids[:, None]).astype(jnp.bfloat16)
        rows = jnp.dot(hits, embeddings, preferred_element_type=jnp.float32).astype(jnp.bfloat16)
        rows = rows.reshape(SPILL, member_count, share // 2, 2).transpose(1, 0, 3, 2)
        rows = rows.reshape(member_count, SPILL, share)
        rows = lax.all_to_all(rows, "group", split_axis=0, concat_axis=0, tiled=True)
        rows = lax.all_gather(rows, "dp", axis=0, tiled=True).reshape(-1, share)
        round_cells = lax.all_gather(tags_at(ids), ("dp", "group"), axis=0, tiled=True)
        round_cells = local_cells(round_cells)
        ones = jnp.ones((rows.shape[0], 128 - share), jnp.float32)
        rows = jnp.concatenate([rows.astype(jnp.float32), ones], axis=1)
        cells = cells.at[round_cells].add(rows)
        sums = sums + jax.ops.segment_sum(rows, round_cells // SUB, num_segments=slots + 1)[:slots]
        return number + 1, cells, sums

    _, cells, sums = lax.while_loop(more, another_round, (jnp.int32(1), cells, sums))

    own = lax.all_to_all(
        sums.reshape(member_count, -1, 128), "group", split_axis=0, concat_axis=0, tiled=True
    )
    fine_update = update(cells, fine_means)
    own_count = own[0, :, share]
    own_sums = own[:, :, :share].reshape(member_count, -1, 2, share // 2)
    own_sums = own_sums.transpose(1, 0, 3, 2).reshape(-1, feature_count)
    coarse_update = (
        (own_sums + coarse_means.astype(jnp.float32)) / (own_count[:, None] + 1.0)
    ).astype(jnp.bfloat16)

    return (coarse_update, fine_update, nearest_cost)


def solution(mesh):
    placed = (
        P(("dp", "group"), None),
        P(("dp", "group")),
        P(("dp", "group")),
        P(),
        P(("dp", "group"), None),
        P("dp", "group"),
    )
    return jax.shard_map(
        on_device,
        mesh=mesh,
        in_specs=placed,
        out_specs=(P(("dp", "group"), None), P("dp", "group"), P(("dp", "group"))),
        check_vma=False,
    )
```

```python
import functools

import jax
import jax.numpy as jnp
from jax import lax
from jax.experimental import pallas as pl
from jax.experimental.pallas import tpu as pltpu
from jax.sharding import PartitionSpec as P

SUB = 64
DIRECT = 32
SPILL = 128
SPILL_FRONT = 96
BATCH = 8
Z_SIZE, Y_SIZE = 8, 4
VMEM_BYTES = 56 * 2**20
MESH = pl.DeviceIdType.MESH


def nt_dot(left, right):
    return lax.dot_general(left, right, (((1,), (1,)), ((), ())), preferred_element_type=jnp.float32)


def pack_kernel(x_ref, position_ref, out_ref, turned):
    features = x_ref.shape[1]
    share = 96
    k = lax.broadcasted_iota(jnp.int32, (features, features), 0)
    within = k % share
    feature = k - within + jnp.where(within < share // 2, 2 * within, 2 * within - share + 1)
    select = feature == lax.broadcasted_iota(jnp.int32, (features, features), 1)
    select = jnp.where(select, 1.0, 0.0).astype(jnp.bfloat16)
    turned[...] = nt_dot(select, x_ref[...]).astype(jnp.bfloat16)
    positions = position_ref[...]
    for tile in range(out_ref.shape[1] // 128):
        ids = tile * 128 + lax.broadcasted_iota(jnp.int32, (128, positions.shape[1]), 0)
        hits = jnp.where(positions == ids, 1.0, 0.0).astype(jnp.bfloat16)
        out_ref[:, tile * 128 : (tile + 1) * 128] = nt_dot(turned[...], hits).astype(jnp.bfloat16)


def pack(embeddings, position, width):
    rows, features = embeddings.shape
    return pl.pallas_call(
        pack_kernel,
        out_shape=jax.ShapeDtypeStruct((features, width), jnp.bfloat16),
        scratch_shapes=[pltpu.VMEM((features, rows), jnp.bfloat16)],
        compiler_params=pltpu.CompilerParams(vmem_limit_bytes=VMEM_BYTES),
    )(embeddings, position.reshape(1, rows))


def regroup_kernel(in_ref, direct_ref, spill_ref):
    members = in_ref.shape[0]
    quads = direct_ref.shape[0] // 4
    to = lax.broadcasted_iota(jnp.int32, (512, 512), 0)
    source = (to // DIRECT) % 4 * 128 + to // 128 * DIRECT + to % DIRECT
    move = source == lax.broadcasted_iota(jnp.int32, (512, 512), 1)
    move = jnp.where(move, 1.0, 0.0).astype(jnp.bfloat16)
    for half in range(members // 4):
        for quad in range(quads):
            block = jnp.concatenate(
                [in_ref[half * 4 + m, :, quad * 128 : (quad + 1) * 128] for m in range(4)], axis=1
            )
            moved = nt_dot(block, move).astype(jnp.bfloat16)
            for i in range(4):
                direct_ref[quad * 4 + i, :, half * 128 : (half + 1) * 128] = moved[
                    :, i * 128 : (i + 1) * 128
                ]
    for m in range(members):
        spill_ref[:, m * SPILL : (m + 1) * SPILL] = in_ref[m, :, quads * 128 :]


def regroup(arrived, owners):
    members, share, _ = arrived.shape
    return pl.pallas_call(
        regroup_kernel,
        out_shape=(
            jax.ShapeDtypeStruct((owners, share, members * DIRECT), jnp.bfloat16),
            jax.ShapeDtypeStruct((share, members * SPILL), jnp.bfloat16),
        ),
        compiler_params=pltpu.CompilerParams(vmem_limit_bytes=VMEM_BYTES),
    )(arrived)


class Rings:
    RATE, LATENCY = 50e3, 2.0

    def __init__(self, planes, send_sem, recv_sem):
        me = lax.axis_index("dp")
        self.z, self.y = me // Y_SIZE, me % Y_SIZE
        self.planes, self.send_sem, self.recv_sem = planes, send_sem, recv_sem
        self.copies, self.count = {}, 0
        z, y = self.z, self.y
        self.sides = {
            "y": (self.owner(z, y + 1), self.owner(z, y - 1)),
            "z": (self.owner(z + 1, y), self.owner(z - 1, y)),
        }

    @staticmethod
    def owner(z_at, y_at):
        return lax.rem(z_at + Z_SIZE, Z_SIZE) * Y_SIZE + lax.rem(y_at + Y_SIZE, Y_SIZE)

    def greet(self):
        barrier = pltpu.get_barrier_semaphore()
        for axis in "yz":
            for side in self.sides[axis]:
                pl.semaphore_signal(barrier, inc=1, device_id={"dp": side}, device_id_type=MESH)

    def at(self, second, back, offset):
        z_shift, y_shift = (-back, offset) if second == "z" else (offset, -back)
        at_z = slice(None) if z_shift is None else lax.rem(self.z + z_shift + Z_SIZE, Z_SIZE)
        at_y = slice(None) if y_shift is None else lax.rem(self.y + y_shift + Y_SIZE, Y_SIZE)
        return (at_z, at_y)

    def send(self, key, source, place, device):
        copy = pltpu.make_async_remote_copy(
            src_ref=source,
            dst_ref=place,
            send_sem=self.send_sem.at[self.count],
            recv_sem=self.recv_sem.at[self.count],
            device_id=device,
            device_id_type=MESH,
        )
        self.count += 1
        copy.start()
        self.copies.setdefault(key, []).append(copy)

    def arrive(self, *key):
        for copy in self.copies[key]:
            copy.wait_recv()

    def jobs(self):
        jobs = {}
        for plane, (_, _, _, _, sizes, eager) in enumerate(self.planes):
            for half in range(2):
                axes = "yz" if half == 0 else "zy"
                lengths = [Y_SIZE if axis == "y" else Z_SIZE for axis in axes]
                for phase in range(2):
                    length = lengths[phase]
                    offsets = [0]
                    if phase == 1:
                        reach = lengths[0] // 2
                        offsets = list(range(1 - reach, reach + 1)) if eager else [None]
                    for offset in offsets:
                        for step in range(1, length // 2 + 1):
                            for side in range(2):
                                if step > 1:
                                    needs = [(plane, half, phase, offset, step - 1, side)]
                                elif phase == 0:
                                    needs = []
                                else:
                                    needs = [
                                        (plane, half, 0, 0, hop, way)
                                        for hop in range(1, reach + 1)
                                        for way in range(2)
                                        if offset is None
                                        or hop == abs(offset) and (hop == reach or (way == 1) == (offset > 0))
                                    ]
                                size = sizes[half] * (0.5 if step == length // 2 else 1.0)
                                if offset is None:
                                    size *= lengths[0]
                                key = (plane, half, phase, offset, step, side)
                                jobs[key] = (needs, axes[phase], step == length // 2, size)
        return jobs

    def start(self, key, axis, last):
        plane, half, phase, offset, step, side = key
        own, everyone, half_index, side_index, _, _ = self.planes[plane]
        index = half_index(half)
        if last:
            index = side_index(side, index)
        other = axis if phase == 1 else ("y" if axis == "z" else "z")
        back = (step - 1) * (1 if side == 0 else -1)
        if phase == 1:
            at = self.at(axis, back, offset)
        else:
            at = self.at(other, 0, -back)
        place = everyone.at[at + index]
        source = own.at[index] if phase == 0 and step == 1 and own is not None else place
        self.send(key, source, place, {"dp": self.sides[axis][side]})

    def run(self, arrived=None, work=(), work_time=0.0, gate=None):
        jobs = self.jobs()
        waiting = sorted(jobs, key=lambda key: (key[2], key[4], key[0], key[1]))
        free, flying, here, work = {}, {}, set(), list(work)
        now = 0.0
        if gate is not None:
            plane, key, time = gate
            for other in waiting:
                if other[0] == plane:
                    jobs[other][0].append(key)
            jobs[key] = ([], None, False, 0.0)
            flying[key] = time
        while waiting or flying:
            for key in list(waiting):
                needs, axis, last, size = jobs[key]
                if all(need in here for need in needs):
                    self.start(key, axis, last)
                    waiting.remove(key)
                    begin = max(now, free.get((axis, key[5]), 0.0))
                    free[(axis, key[5])] = begin + size / self.RATE
                    flying[key] = begin + size / self.RATE + self.LATENCY
            key = min(flying, key=lambda key: (flying[key], jobs[key][3]))
            while work and flying[key] > now + 0.5 * work_time:
                work.pop(0)()
                now += work_time
            now = max(now, flying.pop(key))
            self.arrive(*key)
            here.add(key)
            if arrived is not None:
                arrived(key, here, jobs)
        for item in work:
            item()

    def finish(self):
        for group in self.copies.values():
            for copy in group:
                copy.wait_send()


def spread_kernel(
    block_ref, x_ref, centroids_ref, out_ref, lowest_ref, send_sem, recv_sem, local_sem, doubled, lowest
):
    width = block_ref.shape[1]
    halves = (pl.ds(0, 32), pl.ds(32, 64))
    plane = (
        block_ref,
        out_ref,
        lambda half: (halves[half], pl.ds(0, width)),
        lambda side, index: (index[0], pl.ds(side * width // 2, width // 2)),
        (32 * width * 2, 64 * width * 2),
        True,
    )
    rings = Rings([plane], send_sem, recv_sem)
    rings.greet()
    pl.semaphore_wait(pltpu.get_barrier_semaphore(), 4)
    own = pltpu.make_async_copy(block_ref, out_ref.at[rings.z, rings.y], local_sem)
    own.start()
    own.wait()
    doubled[...] = x_ref[...] * jnp.bfloat16(-2.0)
    lowest[...] = jnp.full_like(lowest, jnp.inf)
    parts = centroids_ref.shape[0] // 256
    share = parts // 8

    def costs(first):
        def piece_costs(part, carry):
            piece = centroids_ref[pl.ds(pl.multiple_of(part * 256, 256), 256), :]
            wide = piece.astype(jnp.float32)
            norms = jnp.sum(wide * wide, axis=1, keepdims=True)
            values = nt_dot(piece, doubled[...]) + norms
            values = jnp.min(values.reshape(32, 8, values.shape[1]), axis=0)
            lowest[...] = jnp.minimum(lowest[...], values)
            return carry

        lax.fori_loop(first, first + share, piece_costs, 0)

    rings.run(None, [functools.partial(costs, i * share) for i in range(8)], 2.2)
    lowest_ref[...] = jnp.min(lowest[...], axis=0, keepdims=True)
    rings.finish()


def spread(block, embeddings, centroids):
    rows, features = embeddings.shape
    out, lowest = pl.pallas_call(
        spread_kernel,
        in_specs=[
            pl.BlockSpec(memory_space=pl.ANY),
            pl.BlockSpec(memory_space=pltpu.VMEM),
            pl.BlockSpec(memory_space=pltpu.VMEM),
        ],
        out_specs=(pl.BlockSpec(memory_space=pl.ANY), pl.BlockSpec(memory_space=pltpu.VMEM)),
        out_shape=(
            jax.ShapeDtypeStruct((Z_SIZE, Y_SIZE) + block.shape, block.dtype),
            jax.ShapeDtypeStruct((1, rows), jnp.float32),
        ),
        scratch_shapes=[
            pltpu.SemaphoreType.DMA((80,)),
            pltpu.SemaphoreType.DMA((80,)),
            pltpu.SemaphoreType.DMA,
            pltpu.VMEM((rows, features), jnp.bfloat16),
            pltpu.VMEM((8, rows), jnp.float32),
        ],
        compiler_params=pltpu.CompilerParams(
            collective_id=0, has_side_effects=True, vmem_limit_bytes=VMEM_BYTES
        ),
        cost_estimate=pl.CostEstimate(
            flops=2 * rows * features * centroids.shape[0], bytes_accessed=2**24, transcendentals=0
        ),
    )(block, embeddings, centroids)
    return out, lowest[0]


def share_kernel(means_ref, tags_ref, all_means, all_tags, send_sem, recv_sem, local_sem):
    member = lax.axis_index("group")
    x, core = member // 2, member % 2
    means, tags = all_means.at[core], all_tags.at[core]

    def plane(everyone, rows, row_bytes, eager):
        return (
            None,
            everyone,
            lambda half: (slice(None), pl.ds(half * rows, rows)),
            lambda side, index: (pl.ds(side * 2, 2), index[1]),
            (4 * rows * row_bytes, 4 * rows * row_bytes),
            eager,
        )

    planes = [plane(means, 16, 1536, True), plane(tags, 8, 512, False)]
    rings = Rings(planes, send_sem, recv_sem)
    sibling = {"group": x * 2 + 1 - core}
    others = [{"group": lax.rem(x + step, 4) * 2 + core} for step in (1, 2, 3)]
    barrier = pltpu.get_barrier_semaphore()
    rings.greet()
    for other in others + [sibling]:
        pl.semaphore_signal(barrier, inc=1, device_id=other, device_id_type=MESH)
    pl.semaphore_wait(barrier, 8)
    z, y = rings.z, rings.y
    blocks = [(means_ref, means.at[z, y]), (tags_ref, tags.at[z, y, x])]
    local = [pltpu.make_async_copy(*block, local_sem.at[i]) for i, block in enumerate(blocks)]
    for copy in local:
        copy.start()
    for other in others:
        rings.send(("x",), *blocks[1], other)
    for copy in local:
        copy.wait()
    sent = set()

    def to_sibling(key, here, jobs):
        if key == ("x",):
            return
        plane, half, phase = key[:3]
        second = "z" if half == 0 else "y"
        reach = (Z_SIZE if second == "z" else Y_SIZE) // 2
        keys = [k for k in jobs if k != ("x",) and k[:2] == (plane, half)]
        for back in range(1 - reach, reach + 1):
            if back == 0:
                needs = [k for k in keys if k[2] == 0] + [("x",)] * plane
            else:
                needs = [
                    k
                    for k in keys
                    if k[2] == 1
                    and k[4] == abs(back)
                    and (abs(back) == reach or (k[5] == 0) == (back > 0))
                ]
            if (plane, half, back) not in sent and all(k in here for k in needs):
                sent.add((plane, half, back))
                _, everyone, half_index, _, _, _ = planes[plane]
                place = everyone.at[rings.at(second, back, None) + half_index(half)]
                rings.send(("core",), place, place, sibling)

    rings.run(to_sibling, gate=(1, ("x",), 20.0))
    rings.arrive("core")
    rings.finish()


def share_all(means, tags):
    any_space = pl.BlockSpec(memory_space=pl.ANY)
    return pl.pallas_call(
        share_kernel,
        in_specs=[any_space, any_space],
        out_specs=(any_space, any_space),
        out_shape=(
            jax.ShapeDtypeStruct((2, Z_SIZE, Y_SIZE) + means.shape, means.dtype),
            jax.ShapeDtypeStruct((2, Z_SIZE, Y_SIZE, 4) + tags.shape, tags.dtype),
        ),
        scratch_shapes=[
            pltpu.SemaphoreType.DMA((160,)),
            pltpu.SemaphoreType.DMA((160,)),
            pltpu.SemaphoreType.DMA((2,)),
        ],
        compiler_params=pltpu.CompilerParams(collective_id=1, has_side_effects=True),
        cost_estimate=pl.CostEstimate(flops=0, bytes_accessed=2**24, transcendentals=0),
    )(means, tags)


def scatter_kernel(direct_steps, tags, flags, direct_ref, spill_ref, cells_ref, sums_ref, other, turned):
    step = pl.program_id(0)
    tables = (cells_ref, other)

    @pl.when(step == 0)
    def _():
        for table in tables:
            table[...] = jnp.zeros_like(table)

    def add_batches(first, end):
        held = None
        for batch in range(first, end + 1):
            fresh = []
            for u in range(BATCH):
                if batch < end:
                    row = u * 128 + batch
                    at = tags[0, 0, row]
                    sums = tables[batch % 2][pl.ds(at, 1), :] + turned[row : row + 1, :]
                    fresh.append((at, sums))
                if held is not None:
                    tables[1 - batch % 2][pl.ds(held[u][0], 1), :] = held[u][1]
            held = fresh

    def add_rows(values, always):
        ones = jnp.ones((32, 128), jnp.float32)
        for block in range(BATCH):
            turned[block * 128 : (block + 1) * 128, :] = jnp.concatenate(
                [values(block).astype(jnp.float32), ones], axis=0
            ).T
        add_batches(0, always)
        if always < 128:

            @pl.when(flags[0, 0, 2] > 0)
            def _():
                add_batches(always, 128)

        def add_repeated(batch, carry):
            for u in range(1, BATCH):
                at = tags[0, 1, u * 128 + batch]
                cells_ref[pl.ds(at, 1), :] += turned[pl.ds(u * 128 + batch, 1), :]
            return carry

        lax.fori_loop(flags[0, 0, 0], flags[0, 0, 1], add_repeated, 0)

    @pl.when(step < direct_steps)
    def _():
        add_rows(lambda block: direct_ref[block // 2, :, block % 2 * 128 : (block % 2 + 1) * 128], 128)

    @pl.when(step >= direct_steps)
    def _():
        add_rows(lambda block: spill_ref[0, :, block * 128 : (block + 1) * 128], SPILL_FRONT)

    @pl.when(step == pl.num_programs(0) - 1)
    def _():
        def slot_sums(group, carry):
            for u in range(8):
                at = pl.ds(pl.multiple_of((group * 8 + u) * SUB, SUB), SUB)
                rows = cells_ref[at, :] + other[at, :]
                cells_ref[at, :] = rows
                sums_ref[pl.ds(group * 8 + u, 1), :] = jnp.sum(rows, axis=0, keepdims=True)
            return carry

        lax.fori_loop(0, sums_ref.shape[0] // 8, slot_sums, 0)


def scatter(tags, direct, spilled, slots):
    direct_steps = direct.shape[0] // 4
    spill_steps = spilled.shape[0]
    share = direct.shape[1]
    steps = direct_steps + spill_steps
    nowhere = slots * SUB
    earlier = jnp.arange(BATCH)[:, None] > jnp.arange(BATCH)[None, :]
    repeated = (tags[:, :, None] == tags[:, None, :]) & earlier[None, :, :, None]
    repeated = jnp.any(repeated, axis=2) & (tags < nowhere)
    planes = jnp.stack(
        [jnp.where(repeated, nowhere, tags), jnp.where(repeated, tags, nowhere)], axis=1
    ).reshape(steps, 2, 1024)
    at_batch = jnp.arange(128, dtype=jnp.int32)
    first = jnp.min(jnp.where(repeated, at_batch, 128), axis=(1, 2))
    last = jnp.max(jnp.where(repeated, at_batch + 1, 0), axis=(1, 2))
    tail = jnp.any(tags[:, :, SPILL_FRONT:] < nowhere, axis=(1, 2)).astype(jnp.int32)
    flags = jnp.stack([first, last, tail], axis=1)
    flags = jnp.pad(flags, ((0, 0), (0, 125))).reshape(steps, 1, 128)
    return pl.pallas_call(
        functools.partial(scatter_kernel, direct_steps),
        grid=(steps,),
        in_specs=[
            pl.BlockSpec((1, 2, 1024), lambda i: (i, 0, 0), memory_space=pltpu.SMEM),
            pl.BlockSpec((1, 1, 128), lambda i: (i, 0, 0), memory_space=pltpu.SMEM),
            pl.BlockSpec((4, share, 256), lambda i: (jnp.minimum(i, direct_steps - 1), 0, 0)),
            pl.BlockSpec((1, share, 1024), lambda i: (jnp.maximum(i - direct_steps, 0), 0, 0)),
        ],
        out_specs=(
            pl.BlockSpec((slots * SUB + 8, 128), lambda i: (0, 0)),
            pl.BlockSpec((slots, 128), lambda i: (0, 0)),
        ),
        out_shape=(
            jax.ShapeDtypeStruct((slots * SUB + 8, 128), jnp.float32),
            jax.ShapeDtypeStruct((slots, 128), jnp.float32),
        ),
        scratch_shapes=[
            pltpu.VMEM((slots * SUB + 8, 128), jnp.float32),
            pltpu.VMEM((1024, 128), jnp.float32),
        ],
        compiler_params=pltpu.CompilerParams(vmem_limit_bytes=VMEM_BYTES),
    )(planes, flags, direct, spilled)


def update_kernel(cells_ref, old_ref, out_ref, turned, counts):
    first = lax.broadcasted_iota(jnp.int32, (48, 128), 1) < SUB
    first_row = first[0:1]
    for pair in range(8):
        block = cells_ref[pair * 128 : (pair + 1) * 128, :].T
        rolled = pltpu.roll(block, SUB, 1)
        even = jnp.where(first, block[0:48], rolled[48:96])
        odd = jnp.where(first, rolled[0:48], block[48:96])
        slot = 2 * pair
        turned[slot // 8, pl.ds(slot % 8, 48, stride=8), :] = even
        turned[slot // 8, pl.ds(slot % 8 + 1, 48, stride=8), :] = odd
        counts[slot : slot + 1, :] = jnp.where(first_row, block[96:97], rolled[96:97])
        counts[slot + 1 : slot + 2, :] = jnp.where(first_row, rolled[96:97], block[96:97])
    scale = 1.0 / (counts[...] + 1.0)
    for tile in range(48):
        sums = jnp.concatenate(
            [turned[0, tile * 8 : (tile + 1) * 8, :], turned[1, tile * 8 : (tile + 1) * 8, :]], axis=0
        )
        old = old_ref[:, tile * 128 : (tile + 1) * 128].astype(jnp.float32)
        out_ref[:, tile * 128 : (tile + 1) * 128] = ((sums + old) * scale).astype(jnp.bfloat16)


def update(cells, fine_means):
    slots, width = fine_means.shape
    return pl.pallas_call(
        update_kernel,
        grid=(slots // 16,),
        in_specs=[
            pl.BlockSpec((16 * SUB, 128), lambda i: (i, 0)),
            pl.BlockSpec((16, width), lambda i: (i, 0)),
        ],
        out_specs=pl.BlockSpec((16, width), lambda i: (i, 0)),
        out_shape=jax.ShapeDtypeStruct((slots, width), jnp.bfloat16),
        scratch_shapes=[pltpu.VMEM((2, 48 * 8, 128), jnp.float32), pltpu.VMEM((16, 128), jnp.float32)],
        compiler_params=pltpu.CompilerParams(vmem_limit_bytes=VMEM_BYTES),
        cost_estimate=pl.CostEstimate(flops=2**24, bytes_accessed=2**24, transcendentals=0),
    )(cells, fine_means)


def on_device(embeddings, coarse_label, fine_label, slot_table, coarse_means, fine_means):
    row_count, feature_count = embeddings.shape
    owner_count = lax.axis_size("dp")
    member_count = lax.axis_size("group")
    slots = fine_means.shape[0]
    share = feature_count // member_count
    table_cells = slots * SUB
    me = lax.axis_index("dp")

    line_means = lax.all_gather(coarse_means, "group", axis=0, tiled=False)
    line_means = line_means.reshape((member_count // 2, 2) + coarse_means.shape)
    line_means = lax.dynamic_index_in_dim(line_means, lax.axis_index("group") % 2, 1, keepdims=False)

    slot_index = jnp.take(slot_table, coarse_label)
    owner_index = slot_index // slots
    matches = owner_index[:, None] == jnp.arange(owner_count, dtype=jnp.int32)[None, :]
    row_ids = jnp.arange(row_count, dtype=jnp.int32)
    before = (row_ids[:, None] > row_ids[None, :]).astype(jnp.bfloat16)
    earlier = jnp.dot(before, matches.astype(jnp.bfloat16), preferred_element_type=jnp.float32)
    excess = jnp.maximum(jnp.sum(matches.astype(jnp.int32), axis=0) - DIRECT, 0)
    owner_ids = jnp.arange(owner_count, dtype=jnp.int32)
    ahead = (excess[None, :] > excess[:, None]) | (
        (excess[None, :] == excess[:, None]) & (owner_ids[None, :] < owner_ids[:, None])
    )
    offsets = jnp.sum(jnp.where(ahead, excess[None, :], 0), axis=1)
    excess_total = jnp.sum(excess)
    rank = jnp.sum(jnp.where(matches, earlier, 0.0), axis=1).astype(jnp.int32)
    offset = jnp.sum(jnp.where(matches, offsets[None, :], 0), axis=1)
    direct_width = owner_count * DIRECT
    position = jnp.where(
        rank < DIRECT, owner_index * DIRECT + rank, direct_width + offset + rank - DIRECT
    )
    cell = slot_index * SUB + fine_label
    width = direct_width + SPILL

    def tags_at(position_ids):
        hits = position[None, :] == position_ids[:, None]
        return jnp.sum(jnp.where(hits, cell[None, :] + 1, 0), axis=1)

    tags = jnp.concatenate(
        [
            tags_at(jnp.arange(width, dtype=jnp.int32)).reshape(-1, 128),
            jnp.broadcast_to(excess_total, (16 - width // 128, 128)),
        ],
        axis=0,
    )
    packed = pack(embeddings, position, width).reshape(member_count, share, width)
    packed, tags = lax.optimization_barrier((packed, tags))
    arrived = lax.all_to_all(packed, "group", split_axis=0, concat_axis=0, tiled=True)
    centroids, all_tags = share_all(line_means, tags)
    arrived, centroids, all_tags = lax.optimization_barrier((arrived, centroids, all_tags))
    direct, spill = regroup(arrived, owner_count)
    direct = lax.all_to_all(direct, "dp", split_axis=0, concat_axis=0, tiled=True)
    own_norms = jnp.sum(jnp.square(embeddings.astype(jnp.float32)), axis=1)
    spilled, lowest = spread(spill, embeddings, centroids.reshape(-1, feature_count))
    spilled = spilled.reshape(owner_count, share, member_count * SPILL)
    nearest_cost = (own_norms + lowest) / feature_count

    def local_cells(global_tags):
        local = global_tags - 1 - me * table_cells
        return jnp.where((local >= 0) & (local < table_cells), local, table_cells)

    all_tags = all_tags.reshape(2, owner_count, 4, 16, 128)
    per_line = 128 // DIRECT
    direct_tags = lax.dynamic_slice_in_dim(all_tags, me // per_line, 1, axis=3)
    direct_tags = lax.dynamic_slice_in_dim(direct_tags, me % per_line * DIRECT, DIRECT, axis=4)
    spill_tags = all_tags[:, :, :, direct_width // 128]
    step_tags = jnp.concatenate(
        [
            direct_tags.reshape(2, owner_count, 4, DIRECT).transpose(1, 2, 0, 3).reshape(-1, 8, 128),
            spill_tags.transpose(1, 2, 0, 3).reshape(-1, 8, 128),
        ],
        axis=0,
    )
    cells, sums = scatter(local_cells(step_tags), direct, spilled, slots)
    rounds = (jnp.max(all_tags[:, :, :, width // 128, 0]) + SPILL - 1) // SPILL

    def more(state):
        return state[0] < rounds

    def another_round(state):
        number, cells, sums = state
        ids = direct_width + number * SPILL + jnp.arange(SPILL, dtype=jnp.int32)
        hits = (position[None, :] == ids[:, None]).astype(jnp.bfloat16)
        rows = jnp.dot(hits, embeddings, preferred_element_type=jnp.float32).astype(jnp.bfloat16)
        rows = rows.reshape(SPILL, member_count, share // 2, 2).transpose(1, 0, 3, 2)
        rows = rows.reshape(member_count, SPILL, share)
        rows = lax.all_to_all(rows, "group", split_axis=0, concat_axis=0, tiled=True)
        rows = lax.all_gather(rows, "dp", axis=0, tiled=True).reshape(-1, share)
        round_cells = lax.all_gather(tags_at(ids), ("dp", "group"), axis=0, tiled=True)
        round_cells = local_cells(round_cells)
        ones = jnp.ones((rows.shape[0], 128 - share), jnp.float32)
        rows = jnp.concatenate([rows.astype(jnp.float32), ones], axis=1)
        cells = cells.at[round_cells].add(rows)
        sums = sums + jax.ops.segment_sum(rows, round_cells // SUB, num_segments=slots + 1)[:slots]
        return number + 1, cells, sums

    _, cells, sums = lax.while_loop(more, another_round, (jnp.int32(1), cells, sums))

    own = lax.all_to_all(
        sums.reshape(member_count, -1, 128), "group", split_axis=0, concat_axis=0, tiled=True
    )
    fine_update = update(cells, fine_means)
    own_count = own[0, :, share]
    own_sums = own[:, :, :share].reshape(member_count, -1, 2, share // 2)
    own_sums = own_sums.transpose(1, 0, 3, 2).reshape(-1, feature_count)
    coarse_update = (
        (own_sums + coarse_means.astype(jnp.float32)) / (own_count[:, None] + 1.0)
    ).astype(jnp.bfloat16)

    return (coarse_update, fine_update, nearest_cost)


def solution(mesh):
    placed = (
        P(("dp", "group"), None),
        P(("dp", "group")),
        P(("dp", "group")),
        P(),
        P(("dp", "group"), None),
        P("dp", "group"),
    )
    return jax.shard_map(
        on_device,
        mesh=mesh,
        in_specs=placed,
        out_specs=(P(("dp", "group"), None), P("dp", "group"), P(("dp", "group"))),
        check_vma=False,
    )
```
